256 devices in a mesh: slab: 8 (over y, core), dom: 32 (over z, x).
Axes of the slice: x: 4, y: 4, z: 8, core: 2. Of those that a mesh axis runs over, the one named last changes fastest.
Arguments:
- reference_blocks: bfloat16 [55296, 2, 128], P('slab'), may hold values from -6 to 6
- corner_maps: bfloat16 [8, 128, 128], replicated, may hold values from -0.1875 to 0.1875
- volumes: bfloat16 [256, 32, 32, 32], P(('slab', 'dom')), may hold values from -6 to 6
- wedge: int32 [256, 32768], P(('slab', 'dom')), may hold values 0 or 1
- source_slab: int32 [256, 8, 256, 1], P(('slab', 'dom')), may hold values from 0 to 7; in each aligned block of 256 rows (0 to 255, 256 to 511, ..., all dimensions but the last counted through in order) at most 64 rows name the same one
- block_offset: int32 [256, 8, 256], P(('slab', 'dom')), may hold values from 0 to 6911
- flags: int32 [256], P(('slab', 'dom')), may hold values 0 or 1
- shifts: float32 [256, 24], P(('slab', 'dom')), may hold values from -2 to 2
- past_steps: float32 [4, 256, 24], P(None, ('slab', 'dom')), may hold values from -12 to 12
- past_changes: float32 [4, 256, 24], P(None, ('slab', 'dom')), may hold values from -30 to 30
Outputs:
- scores: float32 [256, 8], P(('slab', 'dom'))
- new_shifts: float32 [256, 24], P(('slab', 'dom'))
The draws below stay inside these ranges and needn't reach their ends.
Inputs may be any that keep to these rules, and one draw needn't show every extreme that they name: `source_slab`: in the 256 blocks of one particle's trial at most 64 name one slab, and some trials name one slab exactly 64 times.
All inputs are finite; a program needn't handle non-finite values. No bound on the sum of `wedge` or of `flags` on one device may be relied on, other than what follows from the above.
Results may differ from the reference program's by a relative error of at most 0.0028.
Values may be sent and summed in bfloat16 or wider, within the bound.
A program may use at most 128 MiB of HBM per device.

```python
import math
import jax
import jax.numpy as jnp
import numpy as np
from jax import lax

BOX = 32
TRIALS = 8
CORNERS = 8
HIST = 4
BOXBLK = 256
REFBLK = 55296
SLAB_BLK = 6912
CAP = 64
PARTICLES = 256
N_SLAB = 8


def history_pair(key):
    keys = jax.random.split(jax.random.fold_in(key, 7), 4)
    full_shape = (HIST, PARTICLES, 3 * TRIALS)
    base_values = jax.random.truncated_normal(keys[0], -4.0, 4.0, full_shape, jnp.float32)
    positions = jnp.arange(PARTICLES, dtype=jnp.float32) / PARTICLES
    spread = jnp.exp(jax.random.uniform(keys[1], (1, PARTICLES, 1), jnp.float32, 0.0, 1.2))
    steps_drawn = 0.3 * base_values * (3.0 ** positions)[None, :, None] * spread
    curvature = jax.random.uniform(keys[2], full_shape, jnp.float32, 0.5, 2.0)
    noise_part = jax.random.uniform(keys[3], full_shape, jnp.float32, -1.0, 1.0)
    changes_drawn = steps_drawn * curvature + 0.3 * noise_part * jnp.abs(steps_drawn)
    return (steps_drawn, changes_drawn)


def draw_past_steps(key, part):
    return history_pair(key)[0]


def draw_past_changes(key, part):
    return history_pair(key)[1]


def place_ends(array, rng, least, high):
    shape = array.shape
    index_at = [jax.random.randint(jax.random.fold_in(rng, axis), (), 0, shape[axis]) for axis in range(len(shape))]
    array = array.at[tuple(index_at)].set(least)
    longest = shape.index(max(shape))
    index_at[longest] = (index_at[longest] + 1) % shape[longest]
    return array.at[tuple(index_at)].set(high)


def block_levels(own_key, shape, pieces, least, largest):
    level = 1.0
    for position, shards_of in pieces:
        heights = jax.random.uniform(jax.random.fold_in(jax.random.fold_in(own_key, 6), position), (shards_of,), jnp.float32, least / len(pieces), largest / len(pieces))
        level = level * jnp.repeat(jnp.exp(heights), shape[position] // shards_of).reshape((-1,) + (1,) * (len(shape) - 1 - position))
    return level


def shared_out(rng, own, number, rows, number_of, top, limit, lean):
    ranking = jax.random.permutation(rng, number_of)
    packed, ordinary = shares(number_of, rows * top, limit, lean, True), shares(number_of, rows * top, limit, lean, False)
    places = jnp.arange(number_of)

    def named(sizes, rotation):
        used = int((sizes > 0).sum())
        fixed = max(1, used // 4)
        passed = fixed + (places - fixed + rotation * (used - fixed)) % max(1, number_of - fixed)
        return jnp.zeros((number_of,), jnp.int32).at[ranking[jnp.where(places < fixed, places, passed)]].set(jnp.asarray(sizes, jnp.int32))

    sizes = jnp.where(number % 4 == 0, named(packed, number // 4), named(ordinary, number - number // 4 - 1))
    mixed = jax.random.permutation(jax.random.fold_in(own, 3), number_of)
    giver, sink = mixed[0:number_of // 2 * 2:2], mixed[1:number_of // 2 * 2:2]
    room = jnp.minimum(sizes[giver] - 1, limit - sizes[sink]) // 2
    room = jnp.where((giver == ranking[0]) | (sink == ranking[0]) | (sizes[sink] == 0), 0, jnp.maximum(room, 0))
    passed = jax.random.randint(jax.random.fold_in(own, 4), (number_of // 2,), 0, 1 << 20) % (room + 1)
    sizes = sizes.at[giver].add(-passed).at[sink].add(passed)
    members = jnp.searchsorted(jnp.cumsum(sizes), jnp.arange(rows * top), side="right").astype(jnp.int32)
    grid = members.reshape(top, rows).T
    grid = grid[jax.random.permutation(jax.random.fold_in(own, 1), rows)]
    rotation = jax.random.randint(jax.random.fold_in(own, 2), (rows, 1), 0, top)
    return jnp.take_along_axis(grid, (jnp.arange(top)[None, :] + rotation) % top, axis=1)


def shares(amount, total, reach, lean, full):
    weights = [(1 << 20) // math.isqrt(rank ** lean) + 1 for rank in range(1, amount + 1)]
    largest = reach if full else min(reach, max(-(-total // amount), total * weights[0] // sum(weights)))
    least = 1 if total - largest >= amount - 1 else 0
    counts, spare = [largest] + [least] * (amount - 1), total - largest - least * (amount - 1)
    while spare > 0:
        free = [i for i in range(1, amount) if counts[i] < largest] or [i for i in range(1, amount) if counts[i] < reach]
        whole, left = sum([weights[i] for i in free]), spare
        for i in free:
            extra = min(reach - counts[i], max(1, left * weights[i] // whole), spare)
            counts[i] = counts[i] + extra
            spare = spare - extra
    return np.array(counts)


def gaussian(key, dims, width, limit, cuts=(), held_as=jnp.bfloat16):
    array = width * jax.random.normal(key, dims, jnp.float32)
    if cuts:
        array = array * block_levels(key, dims, cuts, -0.22, 0.18)
    return jnp.clip(array, -limit, limit).astype(held_as)


def setup_inputs(seed: int = 0) -> dict:
    seeds = jax.random.split(jax.random.key(seed), 11)
    reference_blocks = gaussian(seeds[0], (REFBLK, 2, 128), 1.0, 6.0, ((0, 8),))
    corner_maps = gaussian(seeds[1], (CORNERS, 128, 128), (128 * CORNERS) ** -0.5, 0.1875)
    volumes = gaussian(seeds[2], (PARTICLES, BOX, BOX, BOX), 1.0, 6.0, ((0, 256),))
    wedge = place_ends((jax.random.randint(seeds[3], (PARTICLES, BOX ** 3), 0, 4) < 3).astype(jnp.int32), jax.random.fold_in(seeds[3], 1), 0, 1)
    source_slab_keys = jax.random.split(jax.random.fold_in(seeds[4], 1), PARTICLES * TRIALS * BOXBLK // BOXBLK)
    source_slab_turns = jax.random.permutation(jax.random.fold_in(seeds[4], 3), PARTICLES * TRIALS * BOXBLK // BOXBLK)
    source_slab = jax.vmap(lambda own, number: shared_out(jax.random.fold_in(seeds[4], 2), own, number, BOXBLK, N_SLAB, 1, CAP, 2))(source_slab_keys, source_slab_turns).reshape((PARTICLES, TRIALS, BOXBLK, 1))
    block_offset = place_ends(jax.random.randint(seeds[5], (PARTICLES, TRIALS, BOXBLK), 0, SLAB_BLK), jax.random.fold_in(seeds[5], 1), 0, SLAB_BLK - 1).astype(jnp.int32)
    flags = place_ends((jax.random.randint(seeds[6], (PARTICLES,), 0, 4) < 1).astype(jnp.int32), jax.random.fold_in(seeds[6], 1), 0, 1)
    shifts = jnp.clip(jax.random.uniform(seeds[7], (PARTICLES, 3 * TRIALS), jnp.float32, -2.0, 2.0) * block_levels(seeds[7], (PARTICLES, 3 * TRIALS), ((0, 256),), -0.4, 0.0), -2.0, 2.0)
    past_steps = draw_past_steps(jax.random.fold_in(seeds[10], 71), 0)
    past_changes = draw_past_changes(jax.random.fold_in(seeds[10], 71), 0)
    return {"reference_blocks": reference_blocks, "corner_maps": corner_maps, "volumes": volumes, "wedge": wedge, "source_slab": source_slab, "block_offset": block_offset, "flags": flags, "shifts": shifts, "past_steps": past_steps, "past_changes": past_changes}


def signed_frequency(edge_len):
    index_line = jnp.arange(edge_len, dtype=jnp.int32)
    return jnp.where(index_line < edge_len // 2, index_line, index_line - edge_len).astype(jnp.float32)

def frequency_grid(edge_len):
    freq_line = signed_frequency(edge_len)
    full_shape = (edge_len, edge_len, edge_len)
    freq_one = jnp.broadcast_to(freq_line[:, None, None], full_shape).reshape(-1)
    freq_two = jnp.broadcast_to(freq_line[None, :, None], full_shape).reshape(-1)
    freq_three = jnp.broadcast_to(freq_line[None, None, :], full_shape).reshape(-1)
    return (freq_one, freq_two, freq_three)

def pose_terms(spectrum_real, spectrum_imag, box_real, box_imag, wedge_weight, shift_trio, freq_one, freq_two, freq_three, edge_len):
    cross_real = spectrum_real * box_real + spectrum_imag * box_imag
    cross_imag = spectrum_real * box_imag - spectrum_imag * box_real
    phase_step = 2.0 * math.pi / edge_len
    phases = phase_step * (freq_one * shift_trio[..., 0:1] + freq_two * shift_trio[..., 1:2] + freq_three * shift_trio[..., 2:3])
    cosines = jnp.cos(phases)
    sines = jnp.sin(phases)
    power_particle = lax.optimization_barrier(jnp.sum(wedge_weight * (spectrum_real * spectrum_real + spectrum_imag * spectrum_imag), axis=-1))
    power_box = lax.optimization_barrier(jnp.sum(wedge_weight * (box_real * box_real + box_imag * box_imag), axis=-1))
    factor = math.sqrt(edge_len ** 3) / jnp.sqrt((power_particle + 1e-06) * (power_box + 1e-06))
    scores = factor * lax.optimization_barrier(jnp.sum(wedge_weight * (cross_real * cosines + cross_imag * sines), axis=-1))
    rotation_part = wedge_weight * (cross_imag * cosines - cross_real * sines)
    slopes = jnp.stack([lax.optimization_barrier(jnp.sum(rotation_part * freq_one, axis=-1)), lax.optimization_barrier(jnp.sum(rotation_part * freq_two, axis=-1)), lax.optimization_barrier(jnp.sum(rotation_part * freq_three, axis=-1))], axis=-1)
    return (scores, factor[..., None] * phase_step * slopes)

def reference(reference_blocks, corner_maps, volumes, wedge, source_slab, block_offset, flags, shifts, past_steps, past_changes):
    edge_len = volumes.shape[1]
    freq_one, freq_two, freq_three = frequency_grid(edge_len)

    def one_particle(particle_items):
        slab_ids, offsets, volume, mask_row, shift_row = particle_items
        base_rows = slab_ids[..., 0].astype(jnp.int32) * SLAB_BLK
        summed = jnp.zeros((TRIALS * BOXBLK * 2, 128), jnp.float32)
        for corner in range(CORNERS):
            row_ids = (base_rows + (offsets + corner) % SLAB_BLK).astype(jnp.int32).reshape(-1)
            picked = jnp.take(reference_blocks, row_ids, axis=0).reshape(-1, 128)
            summed = summed + jnp.dot(picked, corner_maps[corner], preferred_element_type=jnp.float32)
        rounded = lax.optimization_barrier(summed.astype(jnp.bfloat16))
        box_values = rounded.astype(jnp.float32).reshape(TRIALS, BOXBLK, 2, 128)
        box_real = box_values[:, :, 0, :].reshape(TRIALS, -1)
        box_imag = box_values[:, :, 1, :].reshape(TRIALS, -1)
        spectrum = jnp.fft.fftn(volume.astype(jnp.float32)).reshape(-1)
        spectrum_real = jnp.real(spectrum).astype(jnp.float32)[None, :]
        spectrum_imag = jnp.imag(spectrum).astype(jnp.float32)[None, :]
        wedge_weight = mask_row.astype(jnp.float32)[None, :]
        return pose_terms(spectrum_real, spectrum_imag, box_real, box_imag, wedge_weight, shift_row.reshape(TRIALS, 3), freq_one, freq_two, freq_three, edge_len)
    scores, slopes = lax.map(one_particle, (source_slab, block_offset, volumes, wedge, shifts))
    active = (1 - flags).astype(jnp.float32)[:, None]
    gradient = -active * slopes.reshape(slopes.shape[0], -1)

    def inner_product(left, right):
        return jnp.sum(left * right)
    inverse_curv = [1.0 / inner_product(past_steps[pair], past_changes[pair]) for pair in range(HIST)]
    alpha_list = [None] * HIST
    direction = gradient
    for pair in reversed(range(HIST)):
        alpha_list[pair] = inverse_curv[pair] * inner_product(past_steps[pair], direction)
        direction = direction - alpha_list[pair] * past_changes[pair]
    scaling = inner_product(past_steps[HIST - 1], past_changes[HIST - 1]) / inner_product(past_changes[HIST - 1], past_changes[HIST - 1])
    result_dir = scaling * direction
    for pair in range(HIST):
        beta_now = inverse_curv[pair] * inner_product(past_changes[pair], result_dir)
        result_dir = result_dir + (alpha_list[pair] - beta_now) * past_steps[pair]
    new_shifts = shifts - active * result_dir
    return (scores, new_shifts)
```

```python
import math

import jax
import jax.numpy as jnp
from jax import lax
from jax.sharding import PartitionSpec as P

CORNERS = 8
HIST = 4
CAP = 64


def signed_frequency(edge_len):
    index_line = jnp.arange(edge_len, dtype=jnp.int32)
    return jnp.where(index_line < edge_len // 2, index_line, index_line - edge_len).astype(
        jnp.float32
    )


def frequency_grid(edge_len):
    freq_line = signed_frequency(edge_len)
    full_shape = (edge_len, edge_len, edge_len)
    freq_one = jnp.broadcast_to(freq_line[:, None, None], full_shape).reshape(-1)
    freq_two = jnp.broadcast_to(freq_line[None, :, None], full_shape).reshape(-1)
    freq_three = jnp.broadcast_to(freq_line[None, None, :], full_shape).reshape(-1)
    return (freq_one, freq_two, freq_three)


def pose_terms(
    spectrum_real,
    spectrum_imag,
    box_real,
    box_imag,
    wedge_weight,
    shift_trio,
    freq_one,
    freq_two,
    freq_three,
    edge_len,
):
    cross_real = spectrum_real * box_real + spectrum_imag * box_imag
    cross_imag = spectrum_real * box_imag - spectrum_imag * box_real
    phase_step = 2.0 * math.pi / edge_len
    phases = phase_step * (
        freq_one * shift_trio[..., 0:1]
        + freq_two * shift_trio[..., 1:2]
        + freq_three * shift_trio[..., 2:3]
    )
    cosines = jnp.cos(phases)
    sines = jnp.sin(phases)
    power_particle = jnp.sum(
        wedge_weight * (spectrum_real * spectrum_real + spectrum_imag * spectrum_imag), axis=-1
    )
    power_box = jnp.sum(wedge_weight * (box_real * box_real + box_imag * box_imag), axis=-1)
    factor = math.sqrt(edge_len**3) / jnp.sqrt((power_particle + 1e-06) * (power_box + 1e-06))
    scores = factor * jnp.sum(wedge_weight * (cross_real * cosines + cross_imag * sines), axis=-1)
    rotation_part = wedge_weight * (cross_imag * cosines - cross_real * sines)
    slopes = jnp.stack(
        [
            jnp.sum(rotation_part * freq_one, axis=-1),
            jnp.sum(rotation_part * freq_two, axis=-1),
            jnp.sum(rotation_part * freq_three, axis=-1),
        ],
        axis=-1,
    )
    return (scores, factor[..., None] * phase_step * slopes)


def fourier_volume(volume):
    edge_len = volume.shape[1]
    highest = lax.Precision.HIGHEST
    index_line = jnp.arange(edge_len, dtype=jnp.int32)
    angles = (
        2.0
        * math.pi
        / edge_len
        * (index_line[:, None] * index_line[None, :] % edge_len).astype(jnp.float32)
    )
    cosine_table = jnp.cos(angles)
    sine_table = jnp.sin(angles)
    real_part = jnp.einsum("ux,pxyz->puyz", cosine_table, volume, precision=highest)
    imag_part = -jnp.einsum("ux,pxyz->puyz", sine_table, volume, precision=highest)
    next_real = jnp.einsum(
        "vy,puyz->puvz", cosine_table, real_part, precision=highest
    ) + jnp.einsum("vy,puyz->puvz", sine_table, imag_part, precision=highest)
    next_imag = jnp.einsum(
        "vy,puyz->puvz", cosine_table, imag_part, precision=highest
    ) - jnp.einsum("vy,puyz->puvz", sine_table, real_part, precision=highest)
    last_real = jnp.einsum(
        "wz,puvz->puvw", cosine_table, next_real, precision=highest
    ) + jnp.einsum("wz,puvz->puvw", sine_table, next_imag, precision=highest)
    last_imag = jnp.einsum(
        "wz,puvz->puvw", cosine_table, next_imag, precision=highest
    ) - jnp.einsum("wz,puvz->puvw", sine_table, next_real, precision=highest)
    return (last_real.reshape(volume.shape[0], -1), last_imag.reshape(volume.shape[0], -1))


def local(
    reference_blocks,
    corner_maps,
    volumes,
    wedge,
    source_slab,
    block_offset,
    flags,
    shifts,
    past_steps,
    past_changes,
):
    local_parts, trials, blocks = block_offset.shape
    slab_len = reference_blocks.shape[0]
    slabs = lax.axis_size("slab")
    own_slab = source_slab[0, :, :, 0]
    offsets = block_offset[0]
    extended = jnp.concatenate([reference_blocks, reference_blocks[: CORNERS - 1]], axis=0)
    summed = jnp.zeros((slab_len * 2, 128), jnp.float32)
    for corner in range(CORNERS):
        summed = summed + jnp.dot(
            extended[corner : corner + slab_len].reshape(-1, 128),
            corner_maps[corner],
            preferred_element_type=jnp.float32,
        )
    mapped = summed.astype(jnp.bfloat16).reshape(slab_len, 256)
    named = (own_slab[:, :, None] == jnp.arange(slabs)[None, None, :]).astype(jnp.int32)
    ranks = jnp.sum((jnp.cumsum(named, axis=1) - named) * named, axis=2)
    slot_of = own_slab * CAP + ranks
    placed = slot_of[:, :, None] == jnp.arange(slabs * CAP)[None, None, :]
    asked = jnp.sum(jnp.where(placed, offsets[:, :, None], 0), axis=1)
    asked = asked.reshape(trials, slabs, CAP).transpose(1, 0, 2)
    wanted = lax.all_to_all(asked, "slab", 0, 0, tiled=True)
    picked = jnp.take(mapped, wanted.reshape(-1), axis=0, mode="clip")
    landed = lax.all_to_all(picked.reshape(slabs, trials * CAP, 256), "slab", 0, 0, tiled=True)
    landed = landed.reshape(slabs, trials, CAP, 256).transpose(1, 0, 2, 3)
    boxes = jnp.einsum(
        "tbk,tkj->tbj",
        placed.astype(jnp.bfloat16),
        landed.reshape(trials, slabs * CAP, 256),
        preferred_element_type=jnp.float32,
    )
    boxes = boxes.reshape(1, trials, blocks, 2, 128)
    edge_len = volumes.shape[1]
    freq_one, freq_two, freq_three = frequency_grid(edge_len)
    spectrum_real, spectrum_imag = fourier_volume(volumes.astype(jnp.float32))
    box_values = boxes.astype(jnp.float32)
    box_real = box_values[:, :, :, 0, :].reshape(local_parts, trials, -1)
    box_imag = box_values[:, :, :, 1, :].reshape(local_parts, trials, -1)
    wedge_weight = wedge.astype(jnp.float32)[:, None, :]
    scores, slopes = pose_terms(
        spectrum_real[:, None, :],
        spectrum_imag[:, None, :],
        box_real,
        box_imag,
        wedge_weight,
        shifts.reshape(local_parts, trials, 3),
        freq_one,
        freq_two,
        freq_three,
        edge_len,
    )
    active = (1 - flags).astype(jnp.float32)[:, None]
    gradient = -active * slopes.reshape(local_parts, -1)
    basis = jnp.concatenate([past_steps[:, 0], past_changes[:, 0], gradient], axis=0)
    gram = lax.psum(jnp.sum(basis[:, None, :] * basis[None, :, :], axis=-1), ("slab", "dom"))
    pair_dots = [gram[pair, HIST + pair] for pair in range(HIST)]
    held = jnp.zeros((2 * HIST + 1,), jnp.float32).at[2 * HIST].set(1.0)
    alpha_list = [None] * HIST
    for pair in reversed(range(HIST)):
        alpha_list[pair] = jnp.sum(gram[pair] * held) / pair_dots[pair]
        held = held.at[HIST + pair].add(-alpha_list[pair])
    held = pair_dots[HIST - 1] / gram[2 * HIST - 1, 2 * HIST - 1] * held
    for pair in range(HIST):
        beta_now = jnp.sum(gram[HIST + pair] * held) / pair_dots[pair]
        held = held.at[pair].add(alpha_list[pair] - beta_now)
    result_dir = jnp.sum(held[:, None] * basis, axis=0)[None]
    new_shifts = shifts - active * result_dir
    return (scores, new_shifts)


def solution(mesh):
    return jax.shard_map(
        local,
        mesh=mesh,
        in_specs=(
            P("slab", None, None),
            P(),
            P(("slab", "dom"), None, None, None),
            P(("slab", "dom"), None),
            P(("slab", "dom"), None, None, None),
            P(("slab", "dom"), None, None),
            P(("slab", "dom")),
            P(("slab", "dom"), None),
            P(None, ("slab", "dom"), None),
            P(None, ("slab", "dom"), None),
        ),
        out_specs=(P(("slab", "dom"), None), P(("slab", "dom"), None)),
        check_vma=False,
    )
```

```python
import functools
import math

import jax
import jax.numpy as jnp
import numpy as np
from jax import lax
from jax.experimental import pallas as pl
from jax.experimental.pallas import tpu as pltpu
from jax.sharding import PartitionSpec as P

CORNERS = 8
HIST = 4
CAP = 64
EDGE = 32
TRIALS = 8
BLOCKS = 256
LANES = 128
SLABS = 8
MESH = pl.DeviceIdType.MESH
CHUNK = 768
F32 = jnp.float32
BF16 = jnp.bfloat16


def split_pair(table):
    high = table.astype(BF16)
    low = (table - high.astype(np.float64)).astype(BF16)
    return np.stack([high, low])


@functools.lru_cache(maxsize=None)
def transform_tables():
    lane = np.arange(LANES)
    row = np.arange(BLOCKS)
    turn = -2j * np.pi
    inner = np.exp(
        turn
        * (
            (lane // 32)[:, None] * (lane // 32)[None, :] / 4
            + (lane % 32)[:, None] * (lane % 32)[None, :] / 32
        )
    )
    twiddle = np.exp(turn * np.arange(8)[:, None] * (lane // 32)[None, :] / 32)
    outer = np.exp(
        turn
        * (
            (row // 8)[:, None] * (row // 8)[None, :] / 32
            + (row % 8)[:, None] * (row % 8)[None, :] / 8
        )
    )
    inner_pair = split_pair(np.concatenate([inner.real, inner.imag], axis=1))
    outer_pair = split_pair(np.concatenate([outer.real, outer.imag], axis=0))
    return inner_pair, outer_pair, np.stack([twiddle.real, twiddle.imag]).astype(np.float32)


def dot(left, right):
    return jnp.dot(left, right, preferred_element_type=F32)


def signed(index):
    return jnp.where(index < EDGE // 2, index, index - EDGE).astype(F32)


def step_kernel(
    rows_ref,
    maps_ref,
    volume_ref,
    wedge_ref,
    slab_ref,
    offset_ref,
    flag_ref,
    shift_smem,
    shift_ref,
    steps_ref,
    changes_ref,
    inner_ref,
    outer_ref,
    twiddle_ref,
    scores_ref,
    new_ref,
    mapped,
    asked_out,
    asked_in,
    asked_smem,
    staged,
    sent,
    landed,
    hot,
    weighted,
    phase_tables,
    line_tables,
    line_smem,
    partial,
    basis,
    sum_slab,
    sum_z,
    sum_x,
    sum_out,
    ask_send,
    ask_recv,
    ask_local,
    data_send,
    data_recv,
    line_local,
    sum_send,
    sum_recv,
):
    slab = lax.axis_index("slab")
    dom = lax.axis_index("dom")
    z_at, x_at = dom // 4, lax.rem(dom, 4)
    slab_peers = [(lax.rem(slab + d, 8), dom) for d in range(1, 8)]
    z_peers = [(slab, lax.rem(z_at + d, 8) * 4 + x_at) for d in range(1, 8)]
    x_peers = [(slab, z_at * 4 + lax.rem(x_at + d, 4)) for d in range(1, 4)]

    barrier = pltpu.get_barrier_semaphore()
    for peer in slab_peers + z_peers + x_peers:
        pl.semaphore_signal(barrier, inc=1, device_id=peer, device_id_type=MESH)

    slab_rows = [slab_ref[t] for t in range(TRIALS)]
    slab_iota = lax.broadcasted_iota(jnp.int32, (SLABS, BLOCKS), 0)
    named = jnp.concatenate(
        [jnp.where(slab_rows[t] == slab_iota, 1.0, 0.0) for t in range(TRIALS)], axis=0
    )
    below = lax.broadcasted_iota(jnp.int32, (BLOCKS, BLOCKS), 0)
    above = lax.broadcasted_iota(jnp.int32, (BLOCKS, BLOCKS), 1)
    before = jnp.where(below < above, 1.0, 0.0).astype(BF16)
    counts = dot(named.astype(BF16), before) * named
    slots = jnp.concatenate(
        [
            slab_rows[t].astype(F32) * CAP
            + jnp.sum(counts[t * SLABS : (t + 1) * SLABS], axis=0, keepdims=True)
            for t in range(TRIALS)
        ],
        axis=0,
    )
    offsets = offset_ref[...]
    high = offsets // LANES
    digits = jnp.concatenate([high, offsets - high * LANES], axis=0).astype(F32).astype(BF16)
    slot_iota = lax.broadcasted_iota(jnp.int32, (SLABS * CAP, BLOCKS), 0).astype(F32)
    trial_iota = lax.broadcasted_iota(jnp.int32, (TRIALS, SLABS * CAP), 0)
    asked = jnp.zeros((TRIALS, SLABS * CAP), F32)
    for t in range(TRIALS):
        placed = jnp.where(slot_iota == slots[t : t + 1], 1.0, 0.0).astype(BF16)
        found = lax.dot_general(
            digits, placed, (((1,), (1,)), ((), ())), preferred_element_type=F32
        )
        asked = jnp.where(
            trial_iota == t, found[:TRIALS] * LANES + found[TRIALS:], asked
        )
    asked = asked.astype(jnp.int32) * 2 + 8
    lane4 = lax.broadcasted_iota(jnp.int32, (4, LANES), 1)
    for s in range(SLABS):
        tile = asked[:, (s // 2) * LANES : (s // 2 + 1) * LANES]
        turned = pltpu.roll(tile, CAP, 1)
        if s % 2 == 0:
            both = jnp.where(lane4 < CAP, tile[:4], turned[4:])
        else:
            both = jnp.where(lane4 < CAP, turned[:4], tile[4:])
        asked_out[s] = jnp.concatenate([both, jnp.zeros((4, LANES), jnp.int32)], axis=0)

    pl.semaphore_wait(barrier, 17)

    def ask(peer):
        return pltpu.make_async_remote_copy(
            src_ref=asked_out.at[peer],
            dst_ref=asked_in.at[slab],
            send_sem=ask_send.at[peer],
            recv_sem=ask_recv.at[slab],
            device_id=(peer, dom),
            device_id_type=MESH,
        )

    for d in range(1, 8):
        ask(lax.rem(slab + d, 8)).start()
    asked_in[slab] = asked_out[slab]

    maps = jnp.concatenate(
        [maps_ref[:4].reshape(512, LANES), maps_ref[4:].reshape(512, LANES)], axis=1
    )
    row_count = rows_ref.shape[0]

    def map_chunk(base, rows):
        wide = jnp.concatenate([rows[2 * m : 2 * m + CHUNK] for m in range(4)], axis=1)
        both = dot(wide, maps)
        mapped[pl.ds(pl.multiple_of(base + 8, 8), CHUNK), :] = both[:, :LANES]
        mapped[pl.ds(pl.multiple_of(base, 8), CHUNK), :] += both[:, LANES:]

    mapped[0:8, :] = jnp.zeros((8, LANES), F32)

    def map_step(i, carry):
        base = pl.multiple_of(i * CHUNK, CHUNK)
        map_chunk(base, rows_ref[pl.ds(base, CHUNK + 16), :])
        return carry

    lax.fori_loop(0, row_count // CHUNK - 1, map_step, 0)
    map_chunk(
        row_count - CHUNK,
        jnp.concatenate([rows_ref[row_count - CHUNK :, :], rows_ref[:16, :]], axis=0),
    )
    mapped[row_count : row_count + 8, :] += mapped[0:8, :]

    for d in range(1, 8):
        peer = lax.rem(slab + d, 8)
        pltpu.make_async_remote_copy(
            src_ref=asked_out.at[peer],
            dst_ref=asked_in.at[peer],
            send_sem=ask_send.at[peer],
            recv_sem=ask_recv.at[peer],
            device_id=(peer, dom),
            device_id_type=MESH,
        ).wait_recv()
    to_smem = pltpu.make_async_copy(asked_in, asked_smem, ask_local)
    to_smem.start()
    to_smem.wait()

    def data(peer, u):
        return pltpu.make_async_remote_copy(
            src_ref=sent.at[peer, u],
            dst_ref=landed.at[slab, u],
            send_sem=data_send.at[peer, u],
            recv_sem=data_recv.at[slab, u],
            device_id=(peer, dom),
            device_id_type=MESH,
        )

    def pick(peer, u):
        for j in range(LANES):
            place = jnp.minimum(jnp.maximum(asked_smem[peer, u, j], 8), row_count + 6)
            staged[2 * j : 2 * j + 2, :] = mapped[pl.ds(place, 2), :]
        return staged[...].astype(BF16)

    def pick_trials(u, carry):
        def pick_peer(d, inner):
            peer = lax.rem(slab + d, 8)
            sent[peer, u] = pick(peer, u)
            data(peer, u).start()
            return inner

        lax.fori_loop(1, 8, pick_peer, 0)
        landed[slab, u] = pick(slab, u)
        return carry

    lax.fori_loop(0, 4, pick_trials, 0)

    volume = volume_ref[0].astype(F32)
    first = jnp.zeros((BLOCKS, 2 * LANES), F32)
    for g in range(4):
        part = volume[:, 8 * g : 8 * g + 8, :].reshape(BLOCKS, EDGE).astype(BF16)
        first = first + dot(part, inner_ref[0, 32 * g : 32 * g + 32, :])
        first = first + dot(part, inner_ref[1, 32 * g : 32 * g + 32, :])
    first = first.reshape(EDGE, 8, 2 * LANES)
    first_r, first_i = first[:, :, :LANES], first[:, :, LANES:]
    turn_r, turn_i = twiddle_ref[0][None], twiddle_ref[1][None]
    second = jnp.concatenate(
        [first_r * turn_r - first_i * turn_i, first_r * turn_i + first_i * turn_r], axis=-1
    ).reshape(BLOCKS, 2 * LANES)
    second_high = second.astype(BF16)
    second_low = (second - second_high.astype(F32)).astype(BF16)
    third = (
        dot(outer_ref[0], second_high)
        + dot(outer_ref[0], second_low)
        + dot(outer_ref[1], second_high)
    )
    spec_r = third[:BLOCKS, :LANES] - third[BLOCKS:, LANES:]
    spec_i = third[:BLOCKS, LANES:] + third[BLOCKS:, :LANES]
    weight = wedge_ref[...].astype(F32)
    weighted[0] = weight * spec_r
    weighted[1] = weight * spec_i
    weighted[2] = weight
    power_particle = jnp.sum(
        jnp.sum(weight * (spec_r * spec_r + spec_i * spec_i), axis=0, keepdims=True),
        axis=1,
        keepdims=True,
    )

    unit = 2.0 * math.pi / EDGE
    sub = lax.broadcasted_iota(jnp.int32, (8, LANES), 0)
    lane = lax.broadcasted_iota(jnp.int32, (8, LANES), 1)
    freq_two = signed(4 * sub + lane // 32)
    freq_three = signed(lane % 32)
    freq_line = signed(lane)
    shift_one = jnp.zeros((8, LANES), F32)
    for t in range(TRIALS):
        angle = unit * (
            freq_two * shift_smem[0, 3 * t + 1] + freq_three * shift_smem[0, 3 * t + 2]
        )
        phase_tables[0, t] = jnp.cos(angle)
        phase_tables[1, t] = jnp.sin(angle)
        shift_one = jnp.where(sub == t, shift_smem[0, 3 * t], shift_one)
    angle = unit * freq_line * shift_one
    cos_line, sin_line = jnp.cos(angle), jnp.sin(angle)
    line_tables[0] = cos_line
    line_tables[1] = sin_line
    line_tables[2] = freq_line * cos_line
    line_tables[3] = freq_line * sin_line
    line_copy = pltpu.make_async_copy(line_tables, line_smem, line_local)
    line_copy.start()

    slot_columns = 2.0 * jnp.transpose(slots)
    hot_iota = lax.broadcasted_iota(jnp.int32, (BLOCKS, SLABS * LANES), 1).astype(F32)
    for t in range(TRIALS):
        column = slot_columns[:, t : t + 1]
        hot[t, :BLOCKS, :] = jnp.where(hot_iota == column, 1.0, 0.0).astype(BF16)
        hot[t, BLOCKS:, :] = jnp.where(hot_iota == column + 1.0, 1.0, 0.0).astype(BF16)

    basis[...] = jnp.zeros((8, LANES), F32)
    for i in range(HIST):
        basis[i : i + 1, : 3 * TRIALS] = steps_ref[i]
        basis[HIST + i : HIST + i + 1, : 3 * TRIALS] = changes_ref[i]
    vectors = basis[...]
    gram = jnp.zeros((8, LANES), F32)
    for j in range(8):
        gram = jnp.where(
            lane == j, jnp.sum(vectors * vectors[j : j + 1], axis=1, keepdims=True), gram
        )
    line_copy.wait()

    def correlate(u, carry):
        for d in range(1, 8):
            peer = lax.rem(slab + d, 8)
            pltpu.make_async_remote_copy(
                src_ref=sent.at[peer, u],
                dst_ref=landed.at[peer, u],
                send_sem=data_send.at[peer, u],
                recv_sem=data_recv.at[peer, u],
                device_id=(peer, dom),
                device_id_type=MESH,
            ).wait_recv()
        for half in range(2):
            t = u + 4 * half
            arrived = landed[:, u, half * LANES : (half + 1) * LANES, :]
            box = dot(hot[t], arrived.reshape(SLABS * LANES, LANES))
            zero = jnp.zeros((8, LANES), F32)
            sum_r, sum_i, line_r, line_i, power = zero, zero, zero, zero, zero
            for k in range(EDGE):
                at = slice(8 * k, 8 * k + 8)
                box_r = box[8 * k : 8 * k + 8]
                box_i = box[BLOCKS + 8 * k : BLOCKS + 8 * k + 8]
                spec_r, spec_i, weight = weighted[0, at], weighted[1, at], weighted[2, at]
                cross_r = spec_r * box_r + spec_i * box_i
                cross_i = spec_r * box_i - spec_i * box_r
                cos_k, sin_k = line_smem[0, t, k], line_smem[1, t, k]
                cos_f, sin_f = line_smem[2, t, k], line_smem[3, t, k]
                sum_r = sum_r + (cross_r * cos_k + cross_i * sin_k)
                sum_i = sum_i + (cross_i * cos_k - cross_r * sin_k)
                line_r = line_r + (cross_r * cos_f + cross_i * sin_f)
                line_i = line_i + (cross_i * cos_f - cross_r * sin_f)
                power = power + weight * (box_r * box_r + box_i * box_i)
            cos_t, sin_t = phase_tables[0, t], phase_tables[1, t]
            real = sum_r * cos_t + sum_i * sin_t
            imag = sum_i * cos_t - sum_r * sin_t
            imag_one = line_i * cos_t - line_r * sin_t
            for n, tile in enumerate(
                (real, imag_one, imag * freq_two, imag * freq_three, power)
            ):
                partial[n, pl.ds(t, 1), :] = jnp.sum(tile, axis=0, keepdims=True)
        return carry

    lax.fori_loop(0, 4, correlate, 0)

    totals = [jnp.sum(partial[n], axis=1, keepdims=True) for n in range(5)]
    factor = math.sqrt(EDGE**3) / jnp.sqrt((power_particle + 1e-06) * (totals[4] + 1e-06))
    scores = jnp.sum(jnp.where(lane == sub, factor * totals[0], 0.0), axis=0, keepdims=True)
    scores_ref[...] = scores[:, :TRIALS]
    active = (1 - flag_ref[0]).astype(F32)
    place = lane - 3 * sub
    slopes = jnp.where(place == 0, totals[1], 0.0)
    slopes = jnp.where(place == 1, totals[2], slopes)
    slopes = jnp.where(place == 2, totals[3], slopes)
    gradient = jnp.sum(-active * (factor * unit) * slopes, axis=0, keepdims=True)
    gram = jnp.where(lane == 8, jnp.sum(vectors * gradient, axis=1, keepdims=True), gram)

    stages = (
        (slab_peers, sum_slab, slab, 0, lambda d: lax.rem(slab + d, 8)),
        (z_peers, sum_z, z_at, 7, lambda d: lax.rem(z_at + d, 8)),
        (x_peers, sum_x, x_at, 14, lambda d: lax.rem(x_at + d, 4)),
    )
    for number, (peers, buffer, own, start, index_of) in enumerate(stages):
        sum_out[number] = gram
        buffer[own] = gram
        size = len(peers) + 1
        for d in range(1, size):
            pltpu.make_async_remote_copy(
                src_ref=sum_out.at[number],
                dst_ref=buffer.at[own],
                send_sem=sum_send.at[start + d - 1],
                recv_sem=sum_recv.at[start + d - 1],
                device_id=peers[d - 1],
                device_id_type=MESH,
            ).start()
        for d in range(1, size):
            pltpu.make_async_remote_copy(
                src_ref=sum_out.at[number],
                dst_ref=buffer.at[index_of(size - d)],
                send_sem=sum_send.at[start + d - 1],
                recv_sem=sum_recv.at[start + d - 1],
                device_id=peers[d - 1],
                device_id_type=MESH,
            ).wait_recv()
        gram = jnp.sum(buffer[...], axis=0)

    lane_row = lane[:1]
    held = jnp.where(lane_row == 2 * HIST, 1.0, 0.0)
    curvature = [gram[i : i + 1, HIST + i : HIST + i + 1] for i in range(HIST)]
    alphas = [None] * HIST
    for i in reversed(range(HIST)):
        alphas[i] = jnp.sum(gram[i : i + 1] * held, axis=1, keepdims=True) / curvature[i]
        held = jnp.where(lane_row == HIST + i, held - alphas[i], held)
    last = 2 * HIST - 1
    gamma = curvature[HIST - 1] / gram[last : last + 1, last : last + 1]
    held = gamma * held
    direction = gradient
    for i in range(HIST):
        direction = direction - alphas[i] * vectors[HIST + i : HIST + i + 1]
    direction = gamma * direction
    for i in range(HIST):
        beta = (
            jnp.sum(gram[HIST + i : HIST + i + 1] * held, axis=1, keepdims=True)
            / curvature[i]
        )
        held = jnp.where(lane_row == i, held + (alphas[i] - beta), held)
        direction = direction + (alphas[i] - beta) * vectors[i : i + 1]
    new_ref[...] = shift_ref[...] - active * direction[:, : 3 * TRIALS]

    for d in range(1, 8):
        ask(lax.rem(slab + d, 8)).wait_send()

    def drain(u, carry):
        for d in range(1, 8):
            data(lax.rem(slab + d, 8), u).wait_send()
        return carry

    lax.fori_loop(0, 4, drain, 0)
    for number, (peers, buffer, own, start, index_of) in enumerate(stages):
        for d in range(1, len(peers) + 1):
            pltpu.make_async_remote_copy(
                src_ref=sum_out.at[number],
                dst_ref=buffer.at[own],
                send_sem=sum_send.at[start + d - 1],
                recv_sem=sum_recv.at[start + d - 1],
                device_id=peers[d - 1],
                device_id_type=MESH,
            ).wait_send()


def local(
    reference_blocks,
    corner_maps,
    volumes,
    wedge,
    source_slab,
    block_offset,
    flags,
    shifts,
    past_steps,
    past_changes,
):
    row_count = reference_blocks.shape[0] * 2
    inner_pair, outer_pair, twiddle = transform_tables()
    vmem = pl.BlockSpec(memory_space=pltpu.VMEM)
    smem = pl.BlockSpec(memory_space=pltpu.SMEM)
    dma = pltpu.SemaphoreType.DMA
    return pl.pallas_call(
        step_kernel,
        out_shape=(
            jax.ShapeDtypeStruct((1, TRIALS), F32),
            jax.ShapeDtypeStruct((1, 3 * TRIALS), F32),
        ),
        in_specs=[vmem] * 6 + [smem, smem] + [vmem] * 6,
        out_specs=(vmem, vmem),
        scratch_shapes=[
            pltpu.VMEM((row_count + 16, LANES), F32),
            pltpu.VMEM((SLABS, 8, LANES), jnp.int32),
            pltpu.VMEM((SLABS, 8, LANES), jnp.int32),
            pltpu.SMEM((SLABS, 8, LANES), jnp.int32),
            pltpu.VMEM((2 * LANES, LANES), F32),
            pltpu.VMEM((SLABS, 4, 2 * LANES, LANES), BF16),
            pltpu.VMEM((SLABS, 4, 2 * LANES, LANES), BF16),
            pltpu.VMEM((TRIALS, 2 * BLOCKS, SLABS * LANES), BF16),
            pltpu.VMEM((3, BLOCKS, LANES), F32),
            pltpu.VMEM((2, TRIALS, 8, LANES), F32),
            pltpu.VMEM((4, TRIALS, LANES), F32),
            pltpu.SMEM((4, TRIALS, LANES), F32),
            pltpu.VMEM((5, TRIALS, LANES), F32),
            pltpu.VMEM((8, LANES), F32),
            pltpu.VMEM((8, 8, LANES), F32),
            pltpu.VMEM((8, 8, LANES), F32),
            pltpu.VMEM((4, 8, LANES), F32),
            pltpu.VMEM((3, 8, LANES), F32),
            dma((8,)),
            dma((8,)),
            dma,
            dma((8, 4)),
            dma((8, 4)),
            dma,
            dma((17,)),
            dma((17,)),
        ],
        compiler_params=pltpu.CompilerParams(
            collective_id=0, has_side_effects=True, vmem_limit_bytes=56 * 2**20
        ),
    )(
        reference_blocks.reshape(row_count, LANES),
        corner_maps,
        volumes,
        wedge.reshape(BLOCKS, LANES),
        source_slab.reshape(TRIALS, 1, BLOCKS),
        block_offset.reshape(TRIALS, BLOCKS),
        flags,
        shifts,
        shifts,
        past_steps,
        past_changes,
        jnp.asarray(inner_pair),
        jnp.asarray(outer_pair),
        jnp.asarray(twiddle),
    )


def solution(mesh):
    return jax.shard_map(
        local,
        mesh=mesh,
        in_specs=(
            P("slab", None, None),
            P(),
            P(("slab", "dom"), None, None, None),
            P(("slab", "dom"), None),
            P(("slab", "dom"), None, None, None),
            P(("slab", "dom"), None, None),
            P(("slab", "dom")),
            P(("slab", "dom"), None),
            P(None, ("slab", "dom"), None),
            P(None, ("slab", "dom"), None),
        ),
        out_specs=(P(("slab", "dom"), None), P(("slab", "dom"), None)),
        check_vma=False,
    )
```

```python
import functools
import math

import jax
import jax.numpy as jnp
import numpy as np
from jax import lax
from jax.experimental import pallas as pl
from jax.experimental.pallas import tpu as pltpu
from jax.sharding import PartitionSpec as P

CORNERS = 8
HIST = 4
CAP = 64
EDGE = 32
TRIALS = 8
BLOCKS = 256
LANES = 128
SLABS = 8
NEAR = 6
MESH = pl.DeviceIdType.MESH
CHUNK = 768
FIRST_CHUNKS = 3
F32 = jnp.float32
BF16 = jnp.bfloat16


def split_pair(table):
    high = table.astype(BF16)
    low = (table - high.astype(np.float64)).astype(BF16)
    return np.stack([high, low])


@functools.lru_cache(maxsize=None)
def transform_tables():
    lane = np.arange(LANES)
    row = np.arange(BLOCKS)
    turn = -2j * np.pi
    inner = np.exp(
        turn
        * (
            (lane // 32)[:, None] * (lane // 32)[None, :] / 4
            + (lane % 32)[:, None] * (lane % 32)[None, :] / 32
        )
    )
    twiddle = np.exp(turn * np.arange(8)[:, None] * (lane // 32)[None, :] / 32)
    outer = np.exp(
        turn
        * (
            (row // 8)[:, None] * (row // 8)[None, :] / 32
            + (row % 8)[:, None] * (row % 8)[None, :] / 8
        )
    )
    inner_pair = split_pair(np.concatenate([inner.real, inner.imag], axis=1))
    outer_pair = split_pair(np.concatenate([outer.real, outer.imag], axis=0))
    return inner_pair, outer_pair, np.stack([twiddle.real, twiddle.imag]).astype(np.float32)


def dot(left, right):
    return jnp.dot(left, right, preferred_element_type=F32)


def signed(index):
    return jnp.where(index < EDGE // 2, index, index - EDGE).astype(F32)


def step_kernel(
    rows_hbm,
    maps_hbm,
    volume_hbm,
    wedge_hbm,
    slab_hbm,
    offset_hbm,
    steps_hbm,
    changes_hbm,
    inner_hbm,
    outer_hbm,
    twiddle_hbm,
    flag_ref,
    shift_smem,
    shift_ref,
    scores_ref,
    new_ref,
    rows_ref,
    maps_ref,
    volume_ref,
    wedge_ref,
    slab_ref,
    offset_ref,
    steps_ref,
    changes_ref,
    inner_ref,
    outer_ref,
    twiddle_ref,
    mapped,
    asked_out,
    asked_in,
    asked_smem,
    staged,
    kept,
    side_out,
    side_in,
    info_out,
    info_in,
    part_out,
    part_in,
    sent,
    landed,
    hot,
    weighted,
    phase_tables,
    line_tables,
    line_smem,
    partial,
    basis,
    sum_slab,
    sum_z,
    sum_x,
    sum_out,
    load_sem,
    ask_send,
    ask_recv,
    ask_local,
    data_send,
    data_recv,
    side_sem,
    info_sem,
    part_sem,
    line_local,
    sum_send,
    sum_recv,
):
    slab = lax.axis_index("slab")
    dom = lax.axis_index("dom")
    z_at, x_at = dom // 4, lax.rem(dom, 4)
    y_at, core = slab // 2, lax.rem(slab, 2)
    near_steps = (1, 2, 6, 7, 3 + 2 * core)
    far = (lax.rem(slab + 4, 8), lax.rem(slab + 5 - 2 * core, 8))

    def place_at(peer):
        step = lax.rem(y_at - peer // 2 + 4, 4)
        return (step - step // 3) * 2 + core

    def place_of(peer):
        step = lax.rem(peer // 2 - y_at + 4, 4)
        return (step - step // 3) * 2 + lax.rem(peer, 2)

    slab_peers = [(lax.rem(slab + d, 8), dom) for d in range(1, 8)]
    z_peers = [(slab, lax.rem(z_at + d, 8) * 4 + x_at) for d in range(1, 8)]
    x_peers = [(slab, z_at * 4 + lax.rem(x_at + d, 4)) for d in range(1, 4)]

    barrier = pltpu.get_barrier_semaphore()
    for peer in slab_peers + z_peers + x_peers:
        pl.semaphore_signal(barrier, inc=1, device_id=peer, device_id_type=MESH)

    pairs = (
        (slab_hbm, slab_ref),
        (offset_hbm, offset_ref),
        (maps_hbm, maps_ref),
        (rows_hbm, rows_ref),
        (volume_hbm, volume_ref),
        (inner_hbm, inner_ref),
        (outer_hbm, outer_ref),
        (twiddle_hbm, twiddle_ref),
        (wedge_hbm, wedge_ref),
        (steps_hbm, steps_ref),
        (changes_hbm, changes_ref),
    )
    loads = [
        pltpu.make_async_copy(source, target, load_sem.at[n])
        for n, (source, target) in enumerate(pairs)
    ]
    for load in loads:
        load.start()
    loads[0].wait()
    loads[1].wait()

    slab_rows = [slab_ref[t] for t in range(TRIALS)]
    slab_iota = lax.broadcasted_iota(jnp.int32, (SLABS, BLOCKS), 0)
    named = jnp.concatenate(
        [jnp.where(slab_rows[t] == slab_iota, 1.0, 0.0) for t in range(TRIALS)], axis=0
    )
    below = lax.broadcasted_iota(jnp.int32, (BLOCKS, BLOCKS), 0)
    above = lax.broadcasted_iota(jnp.int32, (BLOCKS, BLOCKS), 1)
    before = jnp.where(below < above, 1.0, 0.0).astype(BF16)
    counts = dot(named.astype(BF16), before) * named
    slots = jnp.concatenate(
        [
            slab_rows[t].astype(F32) * CAP
            + jnp.sum(counts[t * SLABS : (t + 1) * SLABS], axis=0, keepdims=True)
            for t in range(TRIALS)
        ],
        axis=0,
    )
    offsets = offset_ref[...]
    high = offsets // LANES
    numbers = lax.broadcasted_iota(jnp.int32, (TRIALS, BLOCKS), 1) + 1
    digits = (
        jnp.concatenate([high, offsets - high * LANES, numbers], axis=0)
        .astype(F32)
        .astype(BF16)
    )
    slot_iota = lax.broadcasted_iota(jnp.int32, (SLABS * CAP, BLOCKS), 0).astype(F32)
    trial_iota = lax.broadcasted_iota(jnp.int32, (TRIALS, SLABS * CAP), 0)
    asked = jnp.zeros((TRIALS, SLABS * CAP), F32)
    listed = asked
    for t in range(TRIALS):
        placed = jnp.where(slot_iota == slots[t : t + 1], 1.0, 0.0).astype(BF16)
        found = lax.dot_general(
            digits, placed, (((1,), (1,)), ((), ())), preferred_element_type=F32
        )
        asked = jnp.where(
            trial_iota == t, found[:TRIALS] * LANES + found[TRIALS : 2 * TRIALS], asked
        )
        listed = jnp.where(trial_iota == t, found[2 * TRIALS :], listed)
    asked = asked.astype(jnp.int32) * 2 + 8
    lane4 = lax.broadcasted_iota(jnp.int32, (4, LANES), 1)
    listed = listed.astype(jnp.int32)

    def slab_lanes(table, s):
        tile = table[:, (s // 2) * LANES : (s // 2 + 1) * LANES]
        turned = pltpu.roll(tile, CAP, 1)
        if s % 2 == 0:
            return jnp.where(lane4 < CAP, tile[:4], turned[4:])
        return jnp.where(lane4 < CAP, turned[:4], tile[4:])

    for s in range(SLABS):
        asked_out[s] = jnp.concatenate([slab_lanes(asked, s), slab_lanes(listed, s)], axis=0)

    sub = lax.broadcasted_iota(jnp.int32, (8, LANES), 0)
    lane = lax.broadcasted_iota(jnp.int32, (8, LANES), 1)
    own_shifts = jnp.zeros((8, LANES), F32)
    for t in range(TRIALS):
        for a in range(3):
            own_shifts = jnp.where(
                (sub == t) & (lane == a), shift_smem[0, 3 * t + a], own_shifts
            )
    side_out[...] = own_shifts
    loads[4].wait()
    loads[8].wait()
    volume = volume_ref[0].astype(F32)
    info_out[:BLOCKS, :] = jnp.concatenate(
        [volume[:, 8 * g : 8 * g + 8, :].reshape(BLOCKS, EDGE) for g in range(4)], axis=1
    ).astype(BF16)
    info_out[BLOCKS:, :] = wedge_ref[...].astype(F32).astype(BF16)

    loads[2].wait()
    loads[3].wait()

    maps = jnp.concatenate(
        [maps_ref[:4].reshape(512, LANES), maps_ref[4:].reshape(512, LANES)], axis=1
    )
    row_count = rows_ref.shape[0]

    def map_chunk(base, rows):
        wide = jnp.concatenate([rows[2 * m : 2 * m + CHUNK] for m in range(4)], axis=1)
        both = dot(wide, maps)
        mapped[pl.ds(pl.multiple_of(base + 8, 8), CHUNK), :] = both[:, :LANES]
        mapped[pl.ds(pl.multiple_of(base, 8), CHUNK), :] += both[:, LANES:]

    mapped[0:8, :] = jnp.zeros((8, LANES), F32)

    def map_step(i, carry):
        base = pl.multiple_of(i * CHUNK, CHUNK)
        map_chunk(base, rows_ref[pl.ds(base, CHUNK + 16), :])
        return carry

    lax.fori_loop(0, FIRST_CHUNKS, map_step, 0)

    pl.semaphore_wait(barrier, 17)

    def ask(peer):
        return pltpu.make_async_remote_copy(
            src_ref=asked_out.at[peer],
            dst_ref=asked_in.at[slab],
            send_sem=ask_send.at[peer],
            recv_sem=ask_recv.at[slab],
            device_id=(peer, dom),
            device_id_type=MESH,
        )

    for d in range(1, 8):
        ask(lax.rem(slab + d, 8)).start()

    def far_copy(source, target, sems, which):
        return pltpu.make_async_remote_copy(
            src_ref=source,
            dst_ref=target.at[which],
            send_sem=sems.at[0, which],
            recv_sem=sems.at[1, which],
            device_id=(far[which], dom),
            device_id_type=MESH,
        )

    for which in range(2):
        far_copy(side_out, side_in, side_sem, which).start()
        far_copy(info_out, info_in, info_sem, which).start()

    lax.fori_loop(FIRST_CHUNKS, row_count // CHUNK - 1, map_step, 0)
    map_chunk(
        row_count - CHUNK,
        jnp.concatenate([rows_ref[row_count - CHUNK :, :], rows_ref[:16, :]], axis=0),
    )
    mapped[row_count : row_count + 8, :] += mapped[0:8, :]

    def to_smem(source, peer):
        return pltpu.make_async_copy(source, asked_smem.at[peer], ask_local.at[peer])

    for d in range(1, 8):
        peer = lax.rem(slab + d, 8)
        pltpu.make_async_remote_copy(
            src_ref=asked_out.at[peer],
            dst_ref=asked_in.at[peer],
            send_sem=ask_send.at[peer],
            recv_sem=ask_recv.at[peer],
            device_id=(peer, dom),
            device_id_type=MESH,
        ).wait_recv()
        to_smem(asked_in.at[peer], peer).start()
    to_smem(asked_out.at[slab], slab).start()
    for d in range(1, 8):
        peer = lax.rem(slab + d, 8)
        to_smem(asked_in.at[peer], peer).wait()
    to_smem(asked_out.at[slab], slab).wait()

    def data(peer, u):
        return pltpu.make_async_remote_copy(
            src_ref=sent.at[peer, u],
            dst_ref=landed.at[place_at(peer), u],
            send_sem=data_send.at[peer, u],
            recv_sem=data_recv.at[place_at(peer), u],
            device_id=(peer, dom),
            device_id_type=MESH,
        )

    def pick(peer, u, target):
        for j in range(LANES):
            place = jnp.minimum(jnp.maximum(asked_smem[peer, u, j], 8), row_count + 6)
            target[2 * j : 2 * j + 2, :] = mapped[pl.ds(place, 2), :]

    def pick_trials(u, carry):
        def pick_peer(n, inner):
            step = n + 1 + 3 * (n // 2) - (n // 4) * (8 - 2 * core)
            peer = lax.rem(slab + step, 8)
            pick(peer, u, staged)
            sent[peer, u] = staged[...].astype(BF16)
            data(peer, u).start()
            return inner

        lax.fori_loop(0, 5, pick_peer, 0)
        return carry

    lax.fori_loop(0, 4, pick_trials, 0)

    def pick_own(u, carry):
        pick(slab, u, staged)
        landed[core, u] = staged[...].astype(BF16)
        return carry

    lax.fori_loop(0, 4, pick_own, 0)

    def pick_far(n, carry):
        which, u = n // 4, lax.rem(n, 4)
        pick(lax.rem(slab + 4 + which * (1 - 2 * core), 8), u, kept.at[which, u])
        return carry

    lax.fori_loop(0, 8, pick_far, 0)

    for n in (5, 6, 7, 9, 10):
        loads[n].wait()

    turn_r, turn_i = twiddle_ref[0][None], twiddle_ref[1][None]

    def spectrum(volume_rows):
        first = dot(volume_rows, inner_ref[0]) + dot(volume_rows, inner_ref[1])
        first = first.reshape(EDGE, 8, 2 * LANES)
        first_r, first_i = first[:, :, :LANES], first[:, :, LANES:]
        second = jnp.concatenate(
            [first_r * turn_r - first_i * turn_i, first_r * turn_i + first_i * turn_r],
            axis=-1,
        ).reshape(BLOCKS, 2 * LANES)
        second_high = second.astype(BF16)
        second_low = (second - second_high.astype(F32)).astype(BF16)
        third = (
            dot(outer_ref[0], second_high)
            + dot(outer_ref[0], second_low)
            + dot(outer_ref[1], second_high)
        )
        return (
            third[:BLOCKS, :LANES] - third[BLOCKS:, LANES:],
            third[:BLOCKS, LANES:] + third[BLOCKS:, :LANES],
        )

    spec_r, spec_i = spectrum(info_out[:BLOCKS, :])
    weight = wedge_ref[...].astype(F32)
    weighted[0] = weight * spec_r
    weighted[1] = weight * spec_i
    weighted[2] = weight
    power_particle = jnp.sum(
        jnp.sum(weight * (spec_r * spec_r + spec_i * spec_i), axis=0, keepdims=True),
        axis=1,
        keepdims=True,
    )

    unit = 2.0 * math.pi / EDGE
    freq_two = signed(4 * sub + lane // 32)
    freq_three = signed(lane % 32)
    freq_line = signed(lane)
    shift_one = jnp.zeros((8, LANES), F32)
    for t in range(TRIALS):
        angle = unit * (
            freq_two * shift_smem[0, 3 * t + 1] + freq_three * shift_smem[0, 3 * t + 2]
        )
        phase_tables[0, t] = jnp.cos(angle)
        phase_tables[1, t] = jnp.sin(angle)
        shift_one = jnp.where(sub == t, shift_smem[0, 3 * t], shift_one)
    angle = unit * freq_line * shift_one
    cos_line, sin_line = jnp.cos(angle), jnp.sin(angle)
    line_tables[0] = cos_line
    line_tables[1] = sin_line
    line_tables[2] = freq_line * cos_line
    line_tables[3] = freq_line * sin_line
    line_copy = pltpu.make_async_copy(line_tables, line_smem, line_local)
    line_copy.start()

    place_rows = []
    for t in range(TRIALS):
        step = (slab_rows[t] // 2 - y_at + 4) % 4
        near = jnp.where(step == 3, 2, step) * 2 + slab_rows[t] % 2
        near = jnp.where(step == 2, -2 * SLABS, near - slab_rows[t])
        place_rows.append(slots[t : t + 1] + (CAP * near).astype(F32))
    slot_columns = 2.0 * jnp.transpose(jnp.concatenate(place_rows, axis=0))
    hot_iota = lax.broadcasted_iota(jnp.int32, (BLOCKS, NEAR * LANES), 1).astype(F32)
    for t in range(TRIALS):
        column = slot_columns[:, t : t + 1]
        hot[t, :BLOCKS, :] = jnp.where(hot_iota == column, 1.0, 0.0).astype(BF16)
        hot[t, BLOCKS:, :] = jnp.where(hot_iota == column + 1.0, 1.0, 0.0).astype(BF16)

    basis[...] = jnp.zeros((8, LANES), F32)
    for i in range(HIST):
        basis[i : i + 1, : 3 * TRIALS] = steps_ref[i]
        basis[HIST + i : HIST + i + 1, : 3 * TRIALS] = changes_ref[i]
    vectors = basis[...]
    gram = jnp.zeros((8, LANES), F32)
    for j in range(8):
        gram = jnp.where(
            lane == j, jnp.sum(vectors * vectors[j : j + 1], axis=1, keepdims=True), gram
        )

    block_iota = lax.broadcasted_iota(jnp.int32, (LANES, BLOCKS), 1).astype(F32)
    slot_lane = lax.broadcasted_iota(jnp.int32, (LANES, LANES), 1)
    slot_first = lax.broadcasted_iota(jnp.int32, (LANES, 1), 0) < CAP
    slot_three = signed(slot_lane % 32)
    for which in range(2):
        far_copy(side_out, side_in, side_sem, which).wait_recv()
        far_copy(info_out, info_in, info_sem, which).wait_recv()
        far_r, far_i = spectrum(info_in[which, :BLOCKS, :])
        far_weight = info_in[which, BLOCKS:, :]
        far_r, far_i = far_r * far_weight.astype(F32), far_i * far_weight.astype(F32)
        high_r, high_i = far_r.astype(BF16), far_i.astype(BF16)
        packed = jnp.concatenate(
            [
                high_r,
                high_i,
                (far_r - high_r.astype(F32)).astype(BF16),
                (far_i - high_i.astype(F32)).astype(BF16),
                far_weight,
            ],
            axis=1,
        )
        far_columns = jnp.transpose(asked_in[far[which]].astype(F32)) - 1.0
        far_shifts = side_in[which]
        for u in range(4):
            column = far_columns[:, 4 + u : 5 + u]
            chosen = dot(jnp.where(block_iota == column, 1.0, 0.0).astype(BF16), packed)
            slot_r = chosen[:, :LANES] + chosen[:, 2 * LANES : 3 * LANES]
            slot_i = chosen[:, LANES : 2 * LANES] + chosen[:, 3 * LANES : 4 * LANES]
            slot_weight = chosen[:, 4 * LANES :]
            block = jnp.maximum(column, 0.0).astype(jnp.int32)
            slot_one = signed(block // 8)
            slot_two = signed(4 * (block % 8) + slot_lane // 32)
            trio = [
                jnp.where(
                    slot_first, far_shifts[u : u + 1, a : a + 1], far_shifts[u + 4 : u + 5, a : a + 1]
                )
                for a in range(3)
            ]
            angle = unit * (slot_one * trio[0] + slot_two * trio[1] + slot_three * trio[2])
            cos_s, sin_s = jnp.cos(angle), jnp.sin(angle)
            row_r = kept[which, u, pl.ds(0, LANES, stride=2), :].astype(BF16).astype(F32)
            row_i = kept[which, u, pl.ds(1, LANES, stride=2), :].astype(BF16).astype(F32)
            cross_r = slot_r * row_r + slot_i * row_i
            cross_i = slot_r * row_i - slot_i * row_r
            real = cross_r * cos_s + cross_i * sin_s
            imag = cross_i * cos_s - cross_r * sin_s
            power = slot_weight * (row_r * row_r + row_i * row_i)
            for n, tile in enumerate(
                (real, imag * slot_one, imag * slot_two, imag * slot_three, power)
            ):
                for half in range(2):
                    t = u + 4 * half
                    partial[n, t : t + 1, :] = jnp.sum(
                        tile[half * CAP : (half + 1) * CAP], axis=0, keepdims=True
                    )
        tile = jnp.zeros((8, LANES), F32)
        for n in range(5):
            tile = jnp.where(lane == n, jnp.sum(partial[n], axis=1, keepdims=True), tile)
        part_out[which] = tile
        far_copy(part_out.at[which], part_in, part_sem, which).start()

    line_copy.wait()

    def correlate(u, carry):
        for d in near_steps:
            peer = lax.rem(slab + d, 8)
            pltpu.make_async_remote_copy(
                src_ref=sent.at[peer, u],
                dst_ref=landed.at[place_of(peer), u],
                send_sem=data_send.at[peer, u],
                recv_sem=data_recv.at[place_of(peer), u],
                device_id=(peer, dom),
                device_id_type=MESH,
            ).wait_recv()
        for half in range(2):
            t = u + 4 * half
            arrived = landed[:, u, half * LANES : (half + 1) * LANES, :]
            box = dot(hot[t], arrived.reshape(NEAR * LANES, LANES))
            zero = jnp.zeros((8, LANES), F32)
            sum_r, sum_i, line_r, line_i, power = zero, zero, zero, zero, zero
            for k in range(EDGE):
                at = slice(8 * k, 8 * k + 8)
                box_r = box[8 * k : 8 * k + 8]
                box_i = box[BLOCKS + 8 * k : BLOCKS + 8 * k + 8]
                spec_r, spec_i, weight = weighted[0, at], weighted[1, at], weighted[2, at]
                cross_r = spec_r * box_r + spec_i * box_i
                cross_i = spec_r * box_i - spec_i * box_r
                cos_k, sin_k = line_smem[0, t, k], line_smem[1, t, k]
                cos_f, sin_f = line_smem[2, t, k], line_smem[3, t, k]
                sum_r = sum_r + (cross_r * cos_k + cross_i * sin_k)
                sum_i = sum_i + (cross_i * cos_k - cross_r * sin_k)
                line_r = line_r + (cross_r * cos_f + cross_i * sin_f)
                line_i = line_i + (cross_i * cos_f - cross_r * sin_f)
                power = power + weight * (box_r * box_r + box_i * box_i)
            cos_t, sin_t = phase_tables[0, t], phase_tables[1, t]
            real = sum_r * cos_t + sum_i * sin_t
            imag = sum_i * cos_t - sum_r * sin_t
            imag_one = line_i * cos_t - line_r * sin_t
            for n, tile in enumerate(
                (real, imag_one, imag * freq_two, imag * freq_three, power)
            ):
                partial[n, pl.ds(t, 1), :] = jnp.sum(tile, axis=0, keepdims=True)
        return carry

    lax.fori_loop(0, 4, correlate, 0)

    for which in range(2):
        far_copy(part_out.at[which], part_in, part_sem, which).wait_recv()
    far_part = part_in[0] + part_in[1]
    totals = [
        jnp.sum(partial[n], axis=1, keepdims=True) + far_part[:, n : n + 1] for n in range(5)
    ]
    factor = math.sqrt(EDGE**3) / jnp.sqrt((power_particle + 1e-06) * (totals[4] + 1e-06))
    scores = jnp.sum(jnp.where(lane == sub, factor * totals[0], 0.0), axis=0, keepdims=True)
    scores_ref[...] = scores[:, :TRIALS]
    active = (1 - flag_ref[0]).astype(F32)
    place = lane - 3 * sub
    slopes = jnp.where(place == 0, totals[1], 0.0)
    slopes = jnp.where(place == 1, totals[2], slopes)
    slopes = jnp.where(place == 2, totals[3], slopes)
    gradient = jnp.sum(-active * (factor * unit) * slopes, axis=0, keepdims=True)
    gram = jnp.where(lane == 8, jnp.sum(vectors * gradient, axis=1, keepdims=True), gram)

    stages = (
        (slab_peers, sum_slab, slab, 0, lambda d: lax.rem(slab + d, 8)),
        (z_peers, sum_z, z_at, 7, lambda d: lax.rem(z_at + d, 8)),
        (x_peers, sum_x, x_at, 14, lambda d: lax.rem(x_at + d, 4)),
    )
    for number, (peers, buffer, own, start, index_of) in enumerate(stages):
        sum_out[number] = gram
        buffer[own] = gram
        size = len(peers) + 1
        for d in range(1, size):
            pltpu.make_async_remote_copy(
                src_ref=sum_out.at[number],
                dst_ref=buffer.at[own],
                send_sem=sum_send.at[start + d - 1],
                recv_sem=sum_recv.at[start + d - 1],
                device_id=peers[d - 1],
                device_id_type=MESH,
            ).start()
        for d in range(1, size):
            pltpu.make_async_remote_copy(
                src_ref=sum_out.at[number],
                dst_ref=buffer.at[index_of(size - d)],
                send_sem=sum_send.at[start + d - 1],
                recv_sem=sum_recv.at[start + d - 1],
                device_id=peers[d - 1],
                device_id_type=MESH,
            ).wait_recv()
        gram = jnp.sum(buffer[...], axis=0)

    lane_row = lane[:1]
    held = jnp.where(lane_row == 2 * HIST, 1.0, 0.0)
    curvature = [gram[i : i + 1, HIST + i : HIST + i + 1] for i in range(HIST)]
    alphas = [None] * HIST
    for i in reversed(range(HIST)):
        alphas[i] = jnp.sum(gram[i : i + 1] * held, axis=1, keepdims=True) / curvature[i]
        held = jnp.where(lane_row == HIST + i, held - alphas[i], held)
    last = 2 * HIST - 1
    gamma = curvature[HIST - 1] / gram[last : last + 1, last : last + 1]
    held = gamma * held
    direction = gradient
    for i in range(HIST):
        direction = direction - alphas[i] * vectors[HIST + i : HIST + i + 1]
    direction = gamma * direction
    for i in range(HIST):
        beta = (
            jnp.sum(gram[HIST + i : HIST + i + 1] * held, axis=1, keepdims=True)
            / curvature[i]
        )
        held = jnp.where(lane_row == i, held + (alphas[i] - beta), held)
        direction = direction + (alphas[i] - beta) * vectors[i : i + 1]
    new_ref[...] = shift_ref[...] - active * direction[:, : 3 * TRIALS]

    for d in range(1, 8):
        ask(lax.rem(slab + d, 8)).wait_send()

    for which in range(2):
        far_copy(side_out, side_in, side_sem, which).wait_send()
        far_copy(info_out, info_in, info_sem, which).wait_send()
        far_copy(part_out.at[which], part_in, part_sem, which).wait_send()

    def drain(u, carry):
        for d in near_steps:
            data(lax.rem(slab + d, 8), u).wait_send()
        return carry

    lax.fori_loop(0, 4, drain, 0)
    for number, (peers, buffer, own, start, index_of) in enumerate(stages):
        for d in range(1, len(peers) + 1):
            pltpu.make_async_remote_copy(
                src_ref=sum_out.at[number],
                dst_ref=buffer.at[own],
                send_sem=sum_send.at[start + d - 1],
                recv_sem=sum_recv.at[start + d - 1],
                device_id=peers[d - 1],
                device_id_type=MESH,
            ).wait_send()


def local(
    reference_blocks,
    corner_maps,
    volumes,
    wedge,
    source_slab,
    block_offset,
    flags,
    shifts,
    past_steps,
    past_changes,
):
    row_count = reference_blocks.shape[0] * 2
    inner_pair, outer_pair, twiddle = transform_tables()
    vmem = pl.BlockSpec(memory_space=pltpu.VMEM)
    smem = pl.BlockSpec(memory_space=pltpu.SMEM)
    hbm = pl.BlockSpec(memory_space=pl.ANY)
    dma = pltpu.SemaphoreType.DMA
    large = (
        reference_blocks.reshape(row_count, LANES),
        corner_maps,
        volumes,
        wedge.reshape(BLOCKS, LANES),
        source_slab.reshape(TRIALS, 1, BLOCKS),
        block_offset.reshape(TRIALS, BLOCKS),
        past_steps,
        past_changes,
        jnp.asarray(inner_pair),
        jnp.asarray(outer_pair),
        jnp.asarray(twiddle),
    )
    return pl.pallas_call(
        step_kernel,
        out_shape=(
            jax.ShapeDtypeStruct((1, TRIALS), F32),
            jax.ShapeDtypeStruct((1, 3 * TRIALS), F32),
        ),
        in_specs=[hbm] * len(large) + [smem, smem, vmem],
        out_specs=(vmem, vmem),
        scratch_shapes=[pltpu.VMEM(a.shape, a.dtype) for a in large]
        + [
            pltpu.VMEM((row_count + 16, LANES), F32),
            pltpu.VMEM((SLABS, 8, LANES), jnp.int32),
            pltpu.VMEM((SLABS, 8, LANES), jnp.int32),
            pltpu.SMEM((SLABS, 8, LANES), jnp.int32),
            pltpu.VMEM((2 * LANES, LANES), F32),
            pltpu.VMEM((2, 4, 2 * LANES, LANES), F32),
            pltpu.VMEM((8, LANES), F32),
            pltpu.VMEM((2, 8, LANES), F32),
            pltpu.VMEM((2 * BLOCKS, LANES), BF16),
            pltpu.VMEM((2, 2 * BLOCKS, LANES), BF16),
            pltpu.VMEM((2, 8, LANES), F32),
            pltpu.VMEM((2, 8, LANES), F32),
            pltpu.VMEM((SLABS, 4, 2 * LANES, LANES), BF16),
            pltpu.VMEM((NEAR, 4, 2 * LANES, LANES), BF16),
            pltpu.VMEM((TRIALS, 2 * BLOCKS, NEAR * LANES), BF16),
            pltpu.VMEM((3, BLOCKS, LANES), F32),
            pltpu.VMEM((2, TRIALS, 8, LANES), F32),
            pltpu.VMEM((4, TRIALS, LANES), F32),
            pltpu.SMEM((4, TRIALS, LANES), F32),
            pltpu.VMEM((5, TRIALS, LANES), F32),
            pltpu.VMEM((8, LANES), F32),
            pltpu.VMEM((8, 8, LANES), F32),
            pltpu.VMEM((8, 8, LANES), F32),
            pltpu.VMEM((4, 8, LANES), F32),
            pltpu.VMEM((3, 8, LANES), F32),
            dma((11,)),
            dma((8,)),
            dma((8,)),
            dma((8,)),
            dma((8, 4)),
            dma((NEAR, 4)),
            dma((2, 2)),
            dma((2, 2)),
            dma((2, 2)),
            dma,
            dma((17,)),
            dma((17,)),
        ],
        compiler_params=pltpu.CompilerParams(
            collective_id=0, has_side_effects=True, vmem_limit_bytes=56 * 2**20
        ),
    )(*large, flags, shifts, shifts)


def solution(mesh):
    return jax.shard_map(
        local,
        mesh=mesh,
        in_specs=(
            P("slab", None, None),
            P(),
            P(("slab", "dom"), None, None, None),
            P(("slab", "dom"), None),
            P(("slab", "dom"), None, None, None),
            P(("slab", "dom"), None, None),
            P(("slab", "dom")),
            P(("slab", "dom"), None),
            P(None, ("slab", "dom"), None),
            P(None, ("slab", "dom"), None),
        ),
        out_specs=(P(("slab", "dom"), None), P(("slab", "dom"), None)),
        check_vma=False,
    )
```

```python
import functools
import math

import jax
import jax.numpy as jnp
import numpy as np
from jax import lax
from jax.experimental import pallas as pl
from jax.experimental.pallas import tpu as pltpu
from jax.sharding import PartitionSpec as P

CORNERS = 8
HIST = 4
CAP = 64
EDGE = 32
TRIALS = 8
BLOCKS = 256
LANES = 128
SLABS = 8
NEAR = 6
MESH = pl.DeviceIdType.MESH
CHUNK = 1728
FIRST_CHUNKS = 2
F32 = jnp.float32
BF16 = jnp.bfloat16


def split_pair(table):
    high = table.astype(BF16)
    low = (table - high.astype(np.float64)).astype(BF16)
    return np.stack([high, low])


@functools.lru_cache(maxsize=None)
def transform_tables():
    lane = np.arange(LANES)
    row = np.arange(BLOCKS)
    turn = -2j * np.pi
    inner = np.exp(
        turn
        * (
            (lane // 32)[:, None] * (lane // 32)[None, :] / 4
            + (lane % 32)[:, None] * (lane % 32)[None, :] / 32
        )
    )
    twiddle = np.exp(turn * np.arange(8)[:, None] * (lane // 32)[None, :] / 32)
    outer = np.exp(
        turn
        * (
            (row // 8)[:, None] * (row // 8)[None, :] / 32
            + (row % 8)[:, None] * (row % 8)[None, :] / 8
        )
    )
    inner_pair = split_pair(np.concatenate([inner.real, inner.imag], axis=1))
    outer_pair = split_pair(np.concatenate([outer.real, outer.imag], axis=0))
    return inner_pair, outer_pair, np.stack([twiddle.real, twiddle.imag]).astype(np.float32)


def dot(left, right):
    return jnp.dot(left, right, preferred_element_type=F32)


def signed(index):
    return jnp.where(index < EDGE // 2, index, index - EDGE).astype(F32)


def step_kernel(
    rows_hbm,
    maps_hbm,
    volume_hbm,
    wedge_hbm,
    slab_hbm,
    offset_hbm,
    steps_hbm,
    changes_hbm,
    inner_hbm,
    outer_hbm,
    twiddle_hbm,
    flag_ref,
    shift_smem,
    shift_ref,
    scores_ref,
    new_ref,
    rows_ref,
    maps_ref,
    volume_ref,
    wedge_ref,
    slab_ref,
    offset_ref,
    steps_ref,
    changes_ref,
    inner_ref,
    outer_ref,
    twiddle_ref,
    mapped,
    asked_out,
    asked_in,
    asked_smem,
    staged,
    kept,
    side_out,
    side_in,
    info_out,
    info_in,
    part_out,
    part_in,
    sent,
    landed,
    hot,
    weighted,
    phase_tables,
    line_tables,
    line_smem,
    partial,
    basis,
    sum_slab,
    sum_z,
    sum_x,
    sum_out,
    load_sem,
    ask_send,
    ask_recv,
    ask_local,
    data_send,
    data_recv,
    side_sem,
    info_sem,
    part_sem,
    line_local,
    sum_send,
    sum_recv,
):
    slab = lax.axis_index("slab")
    dom = lax.axis_index("dom")
    z_at, x_at = dom // 4, lax.rem(dom, 4)
    y_at, core = slab // 2, lax.rem(slab, 2)
    near_steps = (1, 2, 6, 7, 3 + 2 * core)
    far = (lax.rem(slab + 4, 8), lax.rem(slab + 5 - 2 * core, 8))

    def place_at(peer):
        step = lax.rem(y_at - peer // 2 + 4, 4)
        return (step - step // 3) * 2 + core

    def place_of(peer):
        step = lax.rem(peer // 2 - y_at + 4, 4)
        return (step - step // 3) * 2 + lax.rem(peer, 2)

    slab_peers = [(lax.rem(slab + d, 8), dom) for d in range(1, 8)]
    z_peers = [(slab, lax.rem(z_at + d, 8) * 4 + x_at) for d in range(1, 8)]
    x_peers = [(slab, z_at * 4 + lax.rem(x_at + d, 4)) for d in range(1, 4)]

    barrier = pltpu.get_barrier_semaphore()
    for peer in slab_peers + z_peers + x_peers:
        pl.semaphore_signal(barrier, inc=1, device_id=peer, device_id_type=MESH)

    pairs = (
        (slab_hbm, slab_ref),
        (offset_hbm, offset_ref),
        (maps_hbm, maps_ref),
        (rows_hbm, rows_ref),
        (volume_hbm, volume_ref),
        (inner_hbm, inner_ref),
        (outer_hbm, outer_ref),
        (twiddle_hbm, twiddle_ref),
        (wedge_hbm, wedge_ref),
        (steps_hbm, steps_ref),
        (changes_hbm, changes_ref),
    )
    loads = [
        pltpu.make_async_copy(source, target, load_sem.at[n])
        for n, (source, target) in enumerate(pairs)
    ]
    for load in loads:
        load.start()
    loads[0].wait()
    loads[1].wait()

    slab_rows = [slab_ref[t] for t in range(TRIALS)]
    slab_iota = lax.broadcasted_iota(jnp.int32, (SLABS, BLOCKS), 0)
    named = jnp.concatenate(
        [jnp.where(slab_rows[t] == slab_iota, 1.0, 0.0) for t in range(TRIALS)], axis=0
    )
    below = lax.broadcasted_iota(jnp.int32, (BLOCKS, BLOCKS), 0)
    above = lax.broadcasted_iota(jnp.int32, (BLOCKS, BLOCKS), 1)
    before = jnp.where(below < above, 1.0, 0.0).astype(BF16)
    counts = dot(named.astype(BF16), before) * named
    slots = jnp.concatenate(
        [
            slab_rows[t].astype(F32) * CAP
            + jnp.sum(counts[t * SLABS : (t + 1) * SLABS], axis=0, keepdims=True)
            for t in range(TRIALS)
        ],
        axis=0,
    )
    offsets = offset_ref[...]
    high = offsets // LANES
    numbers = lax.broadcasted_iota(jnp.int32, (TRIALS, BLOCKS), 1) + 1
    digits = (
        jnp.concatenate([high, offsets - high * LANES, numbers], axis=0)
        .astype(F32)
        .astype(BF16)
    )
    slot_iota = lax.broadcasted_iota(jnp.int32, (SLABS * CAP, BLOCKS), 0).astype(F32)
    trial_iota = lax.broadcasted_iota(jnp.int32, (TRIALS, SLABS * CAP), 0)
    asked = jnp.zeros((TRIALS, SLABS * CAP), F32)
    listed = asked
    for t in range(TRIALS):
        placed = jnp.where(slot_iota == slots[t : t + 1], 1.0, 0.0).astype(BF16)
        found = lax.dot_general(
            digits, placed, (((1,), (1,)), ((), ())), preferred_element_type=F32
        )
        asked = jnp.where(
            trial_iota == t, found[:TRIALS] * LANES + found[TRIALS : 2 * TRIALS], asked
        )
        listed = jnp.where(trial_iota == t, found[2 * TRIALS :], listed)
    asked = asked.astype(jnp.int32) * 2 + 8
    lane4 = lax.broadcasted_iota(jnp.int32, (4, LANES), 1)
    listed = listed.astype(jnp.int32)

    def slab_lanes(table, s):
        tile = table[:, (s // 2) * LANES : (s // 2 + 1) * LANES]
        turned = pltpu.roll(tile, CAP, 1)
        if s % 2 == 0:
            return jnp.where(lane4 < CAP, tile[:4], turned[4:])
        return jnp.where(lane4 < CAP, turned[:4], tile[4:])

    for s in range(SLABS):
        asked_out[s] = jnp.concatenate([slab_lanes(asked, s), slab_lanes(listed, s)], axis=0)

    sub = lax.broadcasted_iota(jnp.int32, (8, LANES), 0)
    lane = lax.broadcasted_iota(jnp.int32, (8, LANES), 1)
    own_shifts = jnp.zeros((8, LANES), F32)
    for t in range(TRIALS):
        for a in range(3):
            own_shifts = jnp.where(
                (sub == t) & (lane == a), shift_smem[0, 3 * t + a], own_shifts
            )
    side_out[...] = own_shifts
    loads[4].wait()
    loads[8].wait()
    volume = volume_ref[0].astype(F32)
    info_out[:BLOCKS, :] = jnp.concatenate(
        [volume[:, 8 * g : 8 * g + 8, :].reshape(BLOCKS, EDGE) for g in range(4)], axis=1
    ).astype(BF16)
    info_out[BLOCKS:, :] = wedge_ref[...].astype(F32).astype(BF16)

    loads[2].wait()
    loads[3].wait()

    maps = jnp.concatenate(
        [maps_ref[:4].reshape(512, LANES), maps_ref[4:].reshape(512, LANES)], axis=1
    )
    row_count = rows_ref.shape[0]

    def map_chunk(base, rows):
        wide = jnp.concatenate([rows[2 * m : 2 * m + CHUNK] for m in range(4)], axis=1)
        both = dot(wide, maps)
        mapped[pl.ds(pl.multiple_of(base + 8, 8), CHUNK), :] = both[:, :LANES]
        mapped[pl.ds(pl.multiple_of(base, 8), CHUNK), :] += both[:, LANES:]

    mapped[0:8, :] = jnp.zeros((8, LANES), F32)

    def map_step(i, carry):
        base = pl.multiple_of(i * CHUNK, CHUNK)
        map_chunk(base, rows_ref[pl.ds(base, CHUNK + 16), :])
        return carry

    lax.fori_loop(0, FIRST_CHUNKS, map_step, 0)

    pl.semaphore_wait(barrier, 17)

    def ask(peer):
        return pltpu.make_async_remote_copy(
            src_ref=asked_out.at[peer],
            dst_ref=asked_in.at[slab],
            send_sem=ask_send.at[peer],
            recv_sem=ask_recv.at[slab],
            device_id=(peer, dom),
            device_id_type=MESH,
        )

    for d in range(1, 8):
        ask(lax.rem(slab + d, 8)).start()

    def far_copy(source, target, sems, which):
        return pltpu.make_async_remote_copy(
            src_ref=source,
            dst_ref=target.at[which],
            send_sem=sems.at[0, which],
            recv_sem=sems.at[1, which],
            device_id=(far[which], dom),
            device_id_type=MESH,
        )

    for which in range(2):
        far_copy(side_out, side_in, side_sem, which).start()
        far_copy(info_out, info_in, info_sem, which).start()

    lax.fori_loop(FIRST_CHUNKS, row_count // CHUNK - 1, map_step, 0)
    map_chunk(
        row_count - CHUNK,
        jnp.concatenate([rows_ref[row_count - CHUNK :, :], rows_ref[:16, :]], axis=0),
    )
    mapped[row_count : row_count + 8, :] += mapped[0:8, :]

    for n in (5, 6, 7, 9, 10):
        loads[n].wait()

    turn_r, turn_i = twiddle_ref[0][None], twiddle_ref[1][None]

    def spectrum(volume_rows):
        first = dot(volume_rows, inner_ref[0]) + dot(volume_rows, inner_ref[1])
        first = first.reshape(EDGE, 8, 2 * LANES)
        first_r, first_i = first[:, :, :LANES], first[:, :, LANES:]
        second = jnp.concatenate(
            [first_r * turn_r - first_i * turn_i, first_r * turn_i + first_i * turn_r],
            axis=-1,
        ).reshape(BLOCKS, 2 * LANES)
        second_high = second.astype(BF16)
        second_low = (second - second_high.astype(F32)).astype(BF16)
        third = (
            dot(outer_ref[0], second_high)
            + dot(outer_ref[0], second_low)
            + dot(outer_ref[1], second_high)
        )
        return (
            third[:BLOCKS, :LANES] - third[BLOCKS:, LANES:],
            third[:BLOCKS, LANES:] + third[BLOCKS:, :LANES],
        )

    spec_r, spec_i = spectrum(info_out[:BLOCKS, :])
    weight = wedge_ref[...].astype(F32)
    weighted[0] = weight * spec_r
    weighted[1] = weight * spec_i
    weighted[2] = weight
    power_particle = jnp.sum(
        jnp.sum(weight * (spec_r * spec_r + spec_i * spec_i), axis=0, keepdims=True),
        axis=1,
        keepdims=True,
    )

    unit = 2.0 * math.pi / EDGE
    freq_two = signed(4 * sub + lane // 32)
    freq_three = signed(lane % 32)
    freq_line = signed(lane)
    shift_one = jnp.zeros((8, LANES), F32)
    for t in range(TRIALS):
        angle = unit * (
            freq_two * shift_smem[0, 3 * t + 1] + freq_three * shift_smem[0, 3 * t + 2]
        )
        phase_tables[0, t] = jnp.cos(angle)
        phase_tables[1, t] = jnp.sin(angle)
        shift_one = jnp.where(sub == t, shift_smem[0, 3 * t], shift_one)
    angle = unit * freq_line * shift_one
    cos_line, sin_line = jnp.cos(angle), jnp.sin(angle)
    line_tables[0] = cos_line
    line_tables[1] = sin_line
    line_tables[2] = freq_line * cos_line
    line_tables[3] = freq_line * sin_line
    line_copy = pltpu.make_async_copy(line_tables, line_smem, line_local)
    line_copy.start()

    place_rows = []
    for t in range(TRIALS):
        step = (slab_rows[t] // 2 - y_at + 4) % 4
        near = jnp.where(step == 3, 2, step) * 2 + slab_rows[t] % 2
        near = jnp.where(step == 2, -2 * SLABS, near - slab_rows[t])
        place_rows.append(slots[t : t + 1] + (CAP * near).astype(F32))
    slot_columns = 2.0 * jnp.transpose(jnp.concatenate(place_rows, axis=0))
    hot_iota = lax.broadcasted_iota(jnp.int32, (BLOCKS, NEAR * LANES), 1).astype(F32)
    for t in range(TRIALS):
        column = slot_columns[:, t : t + 1]
        hot[t, :BLOCKS, :] = jnp.where(hot_iota == column, 1.0, 0.0).astype(BF16)
        hot[t, BLOCKS:, :] = jnp.where(hot_iota == column + 1.0, 1.0, 0.0).astype(BF16)

    basis[...] = jnp.zeros((8, LANES), F32)
    for i in range(HIST):
        basis[i : i + 1, : 3 * TRIALS] = steps_ref[i]
        basis[HIST + i : HIST + i + 1, : 3 * TRIALS] = changes_ref[i]
    vectors = basis[...]
    gram = jnp.zeros((8, LANES), F32)
    for j in range(8):
        gram = jnp.where(
            lane == j, jnp.sum(vectors * vectors[j : j + 1], axis=1, keepdims=True), gram
        )

    def to_smem(source, peer):
        return pltpu.make_async_copy(source, asked_smem.at[peer], ask_local.at[peer])

    for d in range(1, 8):
        peer = lax.rem(slab + d, 8)
        pltpu.make_async_remote_copy(
            src_ref=asked_out.at[peer],
            dst_ref=asked_in.at[peer],
            send_sem=ask_send.at[peer],
            recv_sem=ask_recv.at[peer],
            device_id=(peer, dom),
            device_id_type=MESH,
        ).wait_recv()
        to_smem(asked_in.at[peer], peer).start()
    to_smem(asked_out.at[slab], slab).start()
    for d in range(1, 8):
        peer = lax.rem(slab + d, 8)
        to_smem(asked_in.at[peer], peer).wait()
    to_smem(asked_out.at[slab], slab).wait()

    def data(peer, u):
        return pltpu.make_async_remote_copy(
            src_ref=sent.at[peer, u],
            dst_ref=landed.at[place_at(peer), u],
            send_sem=data_send.at[peer, u],
            recv_sem=data_recv.at[place_at(peer), u],
            device_id=(peer, dom),
            device_id_type=MESH,
        )

    def pick(peer, u, target):
        for j in range(LANES):
            place = jnp.minimum(jnp.maximum(asked_smem[peer, u, j], 8), row_count + 6)
            target[2 * j : 2 * j + 2, :] = mapped[pl.ds(place, 2), :]

    def pick_trials(u, carry):
        def pick_peer(n, inner):
            step = n + 1 + 3 * (n // 2) - (n // 4) * (8 - 2 * core)
            peer = lax.rem(slab + step, 8)
            pick(peer, u, staged)
            sent[peer, u] = staged[...].astype(BF16)
            data(peer, u).start()
            return inner

        lax.fori_loop(0, 5, pick_peer, 0)
        return carry

    lax.fori_loop(0, 4, pick_trials, 0)

    def pick_own(u, carry):
        pick(slab, u, staged)
        landed[core, u] = staged[...].astype(BF16)
        return carry

    lax.fori_loop(0, 4, pick_own, 0)

    def pick_far(n, carry):
        which, u = n // 4, lax.rem(n, 4)
        pick(lax.rem(slab + 4 + which * (1 - 2 * core), 8), u, kept.at[which, u])
        return carry

    lax.fori_loop(0, 8, pick_far, 0)

    block_iota = lax.broadcasted_iota(jnp.int32, (LANES, BLOCKS), 1).astype(F32)
    slot_lane = lax.broadcasted_iota(jnp.int32, (LANES, LANES), 1)
    slot_first = lax.broadcasted_iota(jnp.int32, (LANES, 1), 0) < CAP
    slot_three = signed(slot_lane % 32)
    for which in range(2):
        far_copy(side_out, side_in, side_sem, which).wait_recv()
        far_copy(info_out, info_in, info_sem, which).wait_recv()
        far_r, far_i = spectrum(info_in[which, :BLOCKS, :])
        far_weight = info_in[which, BLOCKS:, :]
        far_r, far_i = far_r * far_weight.astype(F32), far_i * far_weight.astype(F32)
        high_r, high_i = far_r.astype(BF16), far_i.astype(BF16)
        packed = jnp.concatenate(
            [
                high_r,
                high_i,
                (far_r - high_r.astype(F32)).astype(BF16),
                (far_i - high_i.astype(F32)).astype(BF16),
                far_weight,
            ],
            axis=1,
        )
        far_columns = jnp.transpose(asked_in[far[which]].astype(F32)) - 1.0
        far_shifts = side_in[which]
        for u in range(4):
            column = far_columns[:, 4 + u : 5 + u]
            chosen = dot(jnp.where(block_iota == column, 1.0, 0.0).astype(BF16), packed)
            slot_r = chosen[:, :LANES] + chosen[:, 2 * LANES : 3 * LANES]
            slot_i = chosen[:, LANES : 2 * LANES] + chosen[:, 3 * LANES : 4 * LANES]
            slot_weight = chosen[:, 4 * LANES :]
            block = jnp.maximum(column, 0.0).astype(jnp.int32)
            slot_one = signed(block // 8)
            slot_two = signed(4 * (block % 8) + slot_lane // 32)
            trio = [
                jnp.where(
                    slot_first, far_shifts[u : u + 1, a : a + 1], far_shifts[u + 4 : u + 5, a : a + 1]
                )
                for a in range(3)
            ]
            angle = unit * (slot_one * trio[0] + slot_two * trio[1] + slot_three * trio[2])
            cos_s, sin_s = jnp.cos(angle), jnp.sin(angle)
            row_r = kept[which, u, pl.ds(0, LANES, stride=2), :].astype(BF16).astype(F32)
            row_i = kept[which, u, pl.ds(1, LANES, stride=2), :].astype(BF16).astype(F32)
            cross_r = slot_r * row_r + slot_i * row_i
            cross_i = slot_r * row_i - slot_i * row_r
            real = cross_r * cos_s + cross_i * sin_s
            imag = cross_i * cos_s - cross_r * sin_s
            power = slot_weight * (row_r * row_r + row_i * row_i)
            for n, tile in enumerate(
                (real, imag * slot_one, imag * slot_two, imag * slot_three, power)
            ):
                for half in range(2):
                    t = u + 4 * half
                    partial[n, t : t + 1, :] = jnp.sum(
                        tile[half * CAP : (half + 1) * CAP], axis=0, keepdims=True
                    )
        tile = jnp.zeros((8, LANES), F32)
        for n in range(5):
            tile = jnp.where(lane == n, jnp.sum(partial[n], axis=1, keepdims=True), tile)
        part_out[which] = tile
        far_copy(part_out.at[which], part_in, part_sem, which).start()

    line_copy.wait()

    def correlate(u, carry):
        for d in near_steps:
            peer = lax.rem(slab + d, 8)
            pltpu.make_async_remote_copy(
                src_ref=sent.at[peer, u],
                dst_ref=landed.at[place_of(peer), u],
                send_sem=data_send.at[peer, u],
                recv_sem=data_recv.at[place_of(peer), u],
                device_id=(peer, dom),
                device_id_type=MESH,
            ).wait_recv()
        for half in range(2):
            t = u + 4 * half
            arrived = landed[:, u, half * LANES : (half + 1) * LANES, :]
            box = dot(hot[t], arrived.reshape(NEAR * LANES, LANES))
            zero = jnp.zeros((8, LANES), F32)
            sum_r, sum_i, line_r, line_i, power = zero, zero, zero, zero, zero
            for k in range(EDGE):
                at = slice(8 * k, 8 * k + 8)
                box_r = box[8 * k : 8 * k + 8]
                box_i = box[BLOCKS + 8 * k : BLOCKS + 8 * k + 8]
                spec_r, spec_i, weight = weighted[0, at], weighted[1, at], weighted[2, at]
                cross_r = spec_r * box_r + spec_i * box_i
                cross_i = spec_r * box_i - spec_i * box_r
                cos_k, sin_k = line_smem[0, t, k], line_smem[1, t, k]
                cos_f, sin_f = line_smem[2, t, k], line_smem[3, t, k]
                sum_r = sum_r + (cross_r * cos_k + cross_i * sin_k)
                sum_i = sum_i + (cross_i * cos_k - cross_r * sin_k)
                line_r = line_r + (cross_r * cos_f + cross_i * sin_f)
                line_i = line_i + (cross_i * cos_f - cross_r * sin_f)
                power = power + weight * (box_r * box_r + box_i * box_i)
            cos_t, sin_t = phase_tables[0, t], phase_tables[1, t]
            real = sum_r * cos_t + sum_i * sin_t
            imag = sum_i * cos_t - sum_r * sin_t
            imag_one = line_i * cos_t - line_r * sin_t
            for n, tile in enumerate(
                (real, imag_one, imag * freq_two, imag * freq_three, power)
            ):
                partial[n, pl.ds(t, 1), :] = jnp.sum(tile, axis=0, keepdims=True)
        return carry

    lax.fori_loop(0, 4, correlate, 0)

    for which in range(2):
        far_copy(part_out.at[which], part_in, part_sem, which).wait_recv()
    far_part = part_in[0] + part_in[1]
    totals = [
        jnp.sum(partial[n], axis=1, keepdims=True) + far_part[:, n : n + 1] for n in range(5)
    ]
    factor = math.sqrt(EDGE**3) / jnp.sqrt((power_particle + 1e-06) * (totals[4] + 1e-06))
    scores = jnp.sum(jnp.where(lane == sub, factor * totals[0], 0.0), axis=0, keepdims=True)
    scores_ref[...] = scores[:, :TRIALS]
    active = (1 - flag_ref[0]).astype(F32)
    place = lane - 3 * sub
    slopes = jnp.where(place == 0, totals[1], 0.0)
    slopes = jnp.where(place == 1, totals[2], slopes)
    slopes = jnp.where(place == 2, totals[3], slopes)
    gradient = jnp.sum(-active * (factor * unit) * slopes, axis=0, keepdims=True)
    gram = jnp.where(lane == 8, jnp.sum(vectors * gradient, axis=1, keepdims=True), gram)

    stages = (
        (slab_peers, sum_slab, slab, 0, lambda d: lax.rem(slab + d, 8)),
        (z_peers, sum_z, z_at, 7, lambda d: lax.rem(z_at + d, 8)),
        (x_peers, sum_x, x_at, 14, lambda d: lax.rem(x_at + d, 4)),
    )
    for number, (peers, buffer, own, start, index_of) in enumerate(stages):
        sum_out[number] = gram
        buffer[own] = gram
        size = len(peers) + 1
        for d in range(1, size):
            pltpu.make_async_remote_copy(
                src_ref=sum_out.at[number],
                dst_ref=buffer.at[own],
                send_sem=sum_send.at[start + d - 1],
                recv_sem=sum_recv.at[start + d - 1],
                device_id=peers[d - 1],
                device_id_type=MESH,
            ).start()
        for d in range(1, size):
            pltpu.make_async_remote_copy(
                src_ref=sum_out.at[number],
                dst_ref=buffer.at[index_of(size - d)],
                send_sem=sum_send.at[start + d - 1],
                recv_sem=sum_recv.at[start + d - 1],
                device_id=peers[d - 1],
                device_id_type=MESH,
            ).wait_recv()
        gram = jnp.sum(buffer[...], axis=0)

    lane_row = lane[:1]
    held = jnp.where(lane_row == 2 * HIST, 1.0, 0.0)
    curvature = [gram[i : i + 1, HIST + i : HIST + i + 1] for i in range(HIST)]
    alphas = [None] * HIST
    for i in reversed(range(HIST)):
        alphas[i] = jnp.sum(gram[i : i + 1] * held, axis=1, keepdims=True) / curvature[i]
        held = jnp.where(lane_row == HIST + i, held - alphas[i], held)
    last = 2 * HIST - 1
    gamma = curvature[HIST - 1] / gram[last : last + 1, last : last + 1]
    held = gamma * held
    direction = gradient
    for i in range(HIST):
        direction = direction - alphas[i] * vectors[HIST + i : HIST + i + 1]
    direction = gamma * direction
    for i in range(HIST):
        beta = (
            jnp.sum(gram[HIST + i : HIST + i + 1] * held, axis=1, keepdims=True)
            / curvature[i]
        )
        held = jnp.where(lane_row == i, held + (alphas[i] - beta), held)
        direction = direction + (alphas[i] - beta) * vectors[i : i + 1]
    new_ref[...] = shift_ref[...] - active * direction[:, : 3 * TRIALS]

    for d in range(1, 8):
        ask(lax.rem(slab + d, 8)).wait_send()

    for which in range(2):
        far_copy(side_out, side_in, side_sem, which).wait_send()
        far_copy(info_out, info_in, info_sem, which).wait_send()
        far_copy(part_out.at[which], part_in, part_sem, which).wait_send()

    def drain(u, carry):
        for d in near_steps:
            data(lax.rem(slab + d, 8), u).wait_send()
        return carry

    lax.fori_loop(0, 4, drain, 0)
    for number, (peers, buffer, own, start, index_of) in enumerate(stages):
        for d in range(1, len(peers) + 1):
            pltpu.make_async_remote_copy(
                src_ref=sum_out.at[number],
                dst_ref=buffer.at[own],
                send_sem=sum_send.at[start + d - 1],
                recv_sem=sum_recv.at[start + d - 1],
                device_id=peers[d - 1],
                device_id_type=MESH,
            ).wait_send()


def local(
    reference_blocks,
    corner_maps,
    volumes,
    wedge,
    source_slab,
    block_offset,
    flags,
    shifts,
    past_steps,
    past_changes,
):
    row_count = reference_blocks.shape[0] * 2
    inner_pair, outer_pair, twiddle = transform_tables()
    vmem = pl.BlockSpec(memory_space=pltpu.VMEM)
    smem = pl.BlockSpec(memory_space=pltpu.SMEM)
    hbm = pl.BlockSpec(memory_space=pl.ANY)
    dma = pltpu.SemaphoreType.DMA
    large = (
        reference_blocks.reshape(row_count, LANES),
        corner_maps,
        volumes,
        wedge.reshape(BLOCKS, LANES),
        source_slab.reshape(TRIALS, 1, BLOCKS),
        block_offset.reshape(TRIALS, BLOCKS),
        past_steps,
        past_changes,
        jnp.asarray(inner_pair),
        jnp.asarray(outer_pair),
        jnp.asarray(twiddle),
    )
    return pl.pallas_call(
        step_kernel,
        out_shape=(
            jax.ShapeDtypeStruct((1, TRIALS), F32),
            jax.ShapeDtypeStruct((1, 3 * TRIALS), F32),
        ),
        in_specs=[hbm] * len(large) + [smem, smem, vmem],
        out_specs=(vmem, vmem),
        scratch_shapes=[pltpu.VMEM(a.shape, a.dtype) for a in large]
        + [
            pltpu.VMEM((row_count + 16, LANES), F32),
            pltpu.VMEM((SLABS, 8, LANES), jnp.int32),
            pltpu.VMEM((SLABS, 8, LANES), jnp.int32),
            pltpu.SMEM((SLABS, 8, LANES), jnp.int32),
            pltpu.VMEM((2 * LANES, LANES), F32),
            pltpu.VMEM((2, 4, 2 * LANES, LANES), F32),
            pltpu.VMEM((8, LANES), F32),
            pltpu.VMEM((2, 8, LANES), F32),
            pltpu.VMEM((2 * BLOCKS, LANES), BF16),
            pltpu.VMEM((2, 2 * BLOCKS, LANES), BF16),
            pltpu.VMEM((2, 8, LANES), F32),
            pltpu.VMEM((2, 8, LANES), F32),
            pltpu.VMEM((SLABS, 4, 2 * LANES, LANES), BF16),
            pltpu.VMEM((NEAR, 4, 2 * LANES, LANES), BF16),
            pltpu.VMEM((TRIALS, 2 * BLOCKS, NEAR * LANES), BF16),
            pltpu.VMEM((3, BLOCKS, LANES), F32),
            pltpu.VMEM((2, TRIALS, 8, LANES), F32),
            pltpu.VMEM((4, TRIALS, LANES), F32),
            pltpu.SMEM((4, TRIALS, LANES), F32),
            pltpu.VMEM((5, TRIALS, LANES), F32),
            pltpu.VMEM((8, LANES), F32),
            pltpu.VMEM((8, 8, LANES), F32),
            pltpu.VMEM((8, 8, LANES), F32),
            pltpu.VMEM((4, 8, LANES), F32),
            pltpu.VMEM((3, 8, LANES), F32),
            dma((11,)),
            dma((8,)),
            dma((8,)),
            dma((8,)),
            dma((8, 4)),
            dma((NEAR, 4)),
            dma((2, 2)),
            dma((2, 2)),
            dma((2, 2)),
            dma,
            dma((17,)),
            dma((17,)),
        ],
        compiler_params=pltpu.CompilerParams(
            collective_id=0, has_side_effects=True, vmem_limit_bytes=56 * 2**20
        ),
    )(*large, flags, shifts, shifts)


def solution(mesh):
    return jax.shard_map(
        local,
        mesh=mesh,
        in_specs=(
            P("slab", None, None),
            P(),
            P(("slab", "dom"), None, None, None),
            P(("slab", "dom"), None),
            P(("slab", "dom"), None, None, None),
            P(("slab", "dom"), None, None),
            P(("slab", "dom")),
            P(("slab", "dom"), None),
            P(None, ("slab", "dom"), None),
            P(None, ("slab", "dom"), None),
        ),
        out_specs=(P(("slab", "dom"), None), P(("slab", "dom"), None)),
        check_vma=False,
    )
```

```python
import functools
import math

import jax
import jax.numpy as jnp
import numpy as np
from jax import lax
from jax.experimental import pallas as pl
from jax.experimental.pallas import tpu as pltpu
from jax.sharding import PartitionSpec as P

CORNERS = 8
HIST = 4
CAP = 64
EDGE = 32
TRIALS = 8
BLOCKS = 256
LANES = 128
SLABS = 8
NEAR = 6
MESH = pl.DeviceIdType.MESH
CHUNK = 3456
FIRST_CHUNKS = 1
F32 = jnp.float32
BF16 = jnp.bfloat16


def split_pair(table):
    high = table.astype(BF16)
    low = (table - high.astype(np.float64)).astype(BF16)
    return np.stack([high, low])


@functools.lru_cache(maxsize=None)
def transform_tables():
    lane = np.arange(LANES)
    row = np.arange(BLOCKS)
    turn = -2j * np.pi
    inner = np.exp(
        turn
        * (
            (lane // 32)[:, None] * (lane // 32)[None, :] / 4
            + (lane % 32)[:, None] * (lane % 32)[None, :] / 32
        )
    )
    twiddle = np.exp(turn * np.arange(8)[:, None] * (lane // 32)[None, :] / 32)
    outer = np.exp(
        turn
        * (
            (row // 8)[:, None] * (row // 8)[None, :] / 32
            + (row % 8)[:, None] * (row % 8)[None, :] / 8
        )
    )
    inner_pair = split_pair(np.concatenate([inner.real, inner.imag], axis=1))
    outer_pair = split_pair(np.concatenate([outer.real, outer.imag], axis=0))
    return inner_pair, outer_pair, np.stack([twiddle.real, twiddle.imag]).astype(np.float32)


def dot(left, right):
    return jnp.dot(left, right, preferred_element_type=F32)


def signed(index):
    return jnp.where(index < EDGE // 2, index, index - EDGE).astype(F32)


def step_kernel(
    rows_hbm,
    maps_hbm,
    volume_hbm,
    wedge_hbm,
    slab_hbm,
    offset_hbm,
    steps_hbm,
    changes_hbm,
    inner_hbm,
    outer_hbm,
    twiddle_hbm,
    flag_ref,
    shift_smem,
    shift_ref,
    scores_ref,
    new_ref,
    rows_ref,
    maps_ref,
    volume_ref,
    wedge_ref,
    slab_ref,
    offset_ref,
    steps_ref,
    changes_ref,
    inner_ref,
    outer_ref,
    twiddle_ref,
    mapped,
    asked_out,
    asked_in,
    asked_smem,
    staged,
    kept,
    side_out,
    side_in,
    info_out,
    info_in,
    part_out,
    part_in,
    sent,
    landed,
    hot,
    weighted,
    phase_tables,
    line_tables,
    line_smem,
    partial,
    basis,
    sum_slab,
    sum_z,
    sum_x,
    sum_out,
    load_sem,
    ask_send,
    ask_recv,
    ask_local,
    data_send,
    data_recv,
    side_sem,
    info_sem,
    part_sem,
    line_local,
    sum_send,
    sum_recv,
):
    slab = lax.axis_index("slab")
    dom = lax.axis_index("dom")
    z_at, x_at = dom // 4, lax.rem(dom, 4)
    y_at, core = slab // 2, lax.rem(slab, 2)
    near_steps = (1, 2, 6, 7, 3 + 2 * core)
    far = (lax.rem(slab + 4, 8), lax.rem(slab + 5 - 2 * core, 8))

    def place_at(peer):
        step = lax.rem(y_at - peer // 2 + 4, 4)
        return (step - step // 3) * 2 + core

    def place_of(peer):
        step = lax.rem(peer // 2 - y_at + 4, 4)
        return (step - step // 3) * 2 + lax.rem(peer, 2)

    slab_peers = [(lax.rem(slab + d, 8), dom) for d in range(1, 8)]
    z_peers = [(slab, lax.rem(z_at + d, 8) * 4 + x_at) for d in range(1, 8)]
    x_peers = [(slab, z_at * 4 + lax.rem(x_at + d, 4)) for d in range(1, 4)]

    barrier = pltpu.get_barrier_semaphore()
    for peer in slab_peers + z_peers + x_peers:
        pl.semaphore_signal(barrier, inc=1, device_id=peer, device_id_type=MESH)

    pairs = (
        (slab_hbm, slab_ref),
        (offset_hbm, offset_ref),
        (maps_hbm, maps_ref),
        (rows_hbm, rows_ref),
        (volume_hbm, volume_ref),
        (inner_hbm, inner_ref),
        (outer_hbm, outer_ref),
        (twiddle_hbm, twiddle_ref),
        (wedge_hbm, wedge_ref),
        (steps_hbm, steps_ref),
        (changes_hbm, changes_ref),
    )
    loads = [
        pltpu.make_async_copy(source, target, load_sem.at[n])
        for n, (source, target) in enumerate(pairs)
    ]
    for load in loads:
        load.start()
    loads[0].wait()
    loads[1].wait()

    slab_rows = [slab_ref[t] for t in range(TRIALS)]
    slab_iota = lax.broadcasted_iota(jnp.int32, (SLABS, BLOCKS), 0)
    named = jnp.concatenate(
        [jnp.where(slab_rows[t] == slab_iota, 1.0, 0.0) for t in range(TRIALS)], axis=0
    )
    below = lax.broadcasted_iota(jnp.int32, (BLOCKS, BLOCKS), 0)
    above = lax.broadcasted_iota(jnp.int32, (BLOCKS, BLOCKS), 1)
    before = jnp.where(below < above, 1.0, 0.0).astype(BF16)
    counts = dot(named.astype(BF16), before) * named
    slots = jnp.concatenate(
        [
            slab_rows[t].astype(F32) * CAP
            + jnp.sum(counts[t * SLABS : (t + 1) * SLABS], axis=0, keepdims=True)
            for t in range(TRIALS)
        ],
        axis=0,
    )
    offsets = offset_ref[...]
    high = offsets // LANES
    numbers = lax.broadcasted_iota(jnp.int32, (TRIALS, BLOCKS), 1) + 1
    digits = (
        jnp.concatenate([high, offsets - high * LANES, numbers], axis=0)
        .astype(F32)
        .astype(BF16)
    )
    slot_iota = lax.broadcasted_iota(jnp.int32, (SLABS * CAP, BLOCKS), 0).astype(F32)
    trial_iota = lax.broadcasted_iota(jnp.int32, (TRIALS, SLABS * CAP), 0)
    asked = jnp.zeros((TRIALS, SLABS * CAP), F32)
    listed = asked
    for t in range(TRIALS):
        placed = jnp.where(slot_iota == slots[t : t + 1], 1.0, 0.0).astype(BF16)
        found = lax.dot_general(
            digits, placed, (((1,), (1,)), ((), ())), preferred_element_type=F32
        )
        asked = jnp.where(
            trial_iota == t, found[:TRIALS] * LANES + found[TRIALS : 2 * TRIALS], asked
        )
        listed = jnp.where(trial_iota == t, found[2 * TRIALS :], listed)
    asked = asked.astype(jnp.int32) * 2 + 8
    lane4 = lax.broadcasted_iota(jnp.int32, (4, LANES), 1)
    listed = listed.astype(jnp.int32)

    def slab_lanes(table, s):
        tile = table[:, (s // 2) * LANES : (s // 2 + 1) * LANES]
        turned = pltpu.roll(tile, CAP, 1)
        if s % 2 == 0:
            return jnp.where(lane4 < CAP, tile[:4], turned[4:])
        return jnp.where(lane4 < CAP, turned[:4], tile[4:])

    for s in range(SLABS):
        asked_out[s] = jnp.concatenate([slab_lanes(asked, s), slab_lanes(listed, s)], axis=0)

    sub = lax.broadcasted_iota(jnp.int32, (8, LANES), 0)
    lane = lax.broadcasted_iota(jnp.int32, (8, LANES), 1)
    own_shifts = jnp.zeros((8, LANES), F32)
    for t in range(TRIALS):
        for a in range(3):
            own_shifts = jnp.where(
                (sub == t) & (lane == a), shift_smem[0, 3 * t + a], own_shifts
            )
    side_out[...] = own_shifts
    loads[4].wait()
    loads[8].wait()
    volume = volume_ref[0].astype(F32)
    info_out[:BLOCKS, :] = jnp.concatenate(
        [volume[:, 8 * g : 8 * g + 8, :].reshape(BLOCKS, EDGE) for g in range(4)], axis=1
    ).astype(BF16)
    info_out[BLOCKS:, :] = wedge_ref[...].astype(F32).astype(BF16)

    loads[2].wait()
    loads[3].wait()

    maps = jnp.concatenate(
        [maps_ref[:4].reshape(512, LANES), maps_ref[4:].reshape(512, LANES)], axis=1
    )
    row_count = rows_ref.shape[0]

    def map_chunk(base, rows):
        wide = jnp.concatenate([rows[2 * m : 2 * m + CHUNK] for m in range(4)], axis=1)
        both = dot(wide, maps)
        mapped[pl.ds(pl.multiple_of(base + 8, 8), CHUNK), :] = both[:, :LANES]
        mapped[pl.ds(pl.multiple_of(base, 8), CHUNK), :] += both[:, LANES:]

    mapped[0:8, :] = jnp.zeros((8, LANES), F32)

    def map_step(i, carry):
        base = pl.multiple_of(i * CHUNK, CHUNK)
        map_chunk(base, rows_ref[pl.ds(base, CHUNK + 16), :])
        return carry

    lax.fori_loop(0, FIRST_CHUNKS, map_step, 0)

    pl.semaphore_wait(barrier, 17)

    def ask(peer):
        return pltpu.make_async_remote_copy(
            src_ref=asked_out.at[peer],
            dst_ref=asked_in.at[slab],
            send_sem=ask_send.at[peer],
            recv_sem=ask_recv.at[slab],
            device_id=(peer, dom),
            device_id_type=MESH,
        )

    for d in range(1, 8):
        ask(lax.rem(slab + d, 8)).start()

    def far_copy(source, target, sems, which):
        return pltpu.make_async_remote_copy(
            src_ref=source,
            dst_ref=target.at[which],
            send_sem=sems.at[0, which],
            recv_sem=sems.at[1, which],
            device_id=(far[which], dom),
            device_id_type=MESH,
        )

    for which in range(2):
        far_copy(side_out, side_in, side_sem, which).start()
        far_copy(info_out, info_in, info_sem, which).start()

    lax.fori_loop(FIRST_CHUNKS, row_count // CHUNK - 1, map_step, 0)
    map_chunk(
        row_count - CHUNK,
        jnp.concatenate([rows_ref[row_count - CHUNK :, :], rows_ref[:16, :]], axis=0),
    )
    mapped[row_count : row_count + 8, :] += mapped[0:8, :]

    for n in (5, 6, 7, 9, 10):
        loads[n].wait()

    turn_r, turn_i = twiddle_ref[0][None], twiddle_ref[1][None]

    def spectrum(volume_rows):
        first = dot(volume_rows, inner_ref[0]) + dot(volume_rows, inner_ref[1])
        first = first.reshape(EDGE, 8, 2 * LANES)
        first_r, first_i = first[:, :, :LANES], first[:, :, LANES:]
        second = jnp.concatenate(
            [first_r * turn_r - first_i * turn_i, first_r * turn_i + first_i * turn_r],
            axis=-1,
        ).reshape(BLOCKS, 2 * LANES)
        second_high = second.astype(BF16)
        second_low = (second - second_high.astype(F32)).astype(BF16)
        third = (
            dot(outer_ref[0], second_high)
            + dot(outer_ref[0], second_low)
            + dot(outer_ref[1], second_high)
        )
        return (
            third[:BLOCKS, :LANES] - third[BLOCKS:, LANES:],
            third[:BLOCKS, LANES:] + third[BLOCKS:, :LANES],
        )

    spec_r, spec_i = spectrum(info_out[:BLOCKS, :])
    weight = wedge_ref[...].astype(F32)
    weighted[0] = weight * spec_r
    weighted[1] = weight * spec_i
    weighted[2] = weight
    power_particle = jnp.sum(
        jnp.sum(weight * (spec_r * spec_r + spec_i * spec_i), axis=0, keepdims=True),
        axis=1,
        keepdims=True,
    )

    unit = 2.0 * math.pi / EDGE
    freq_two = signed(4 * sub + lane // 32)
    freq_three = signed(lane % 32)
    freq_line = signed(lane)
    shift_one = jnp.zeros((8, LANES), F32)
    for t in range(TRIALS):
        angle = unit * (
            freq_two * shift_smem[0, 3 * t + 1] + freq_three * shift_smem[0, 3 * t + 2]
        )
        phase_tables[0, t] = jnp.cos(angle)
        phase_tables[1, t] = jnp.sin(angle)
        shift_one = jnp.where(sub == t, shift_smem[0, 3 * t], shift_one)
    angle = unit * freq_line * shift_one
    cos_line, sin_line = jnp.cos(angle), jnp.sin(angle)
    line_tables[0] = cos_line
    line_tables[1] = sin_line
    line_tables[2] = freq_line * cos_line
    line_tables[3] = freq_line * sin_line
    line_copy = pltpu.make_async_copy(line_tables, line_smem, line_local)
    line_copy.start()

    place_rows = []
    for t in range(TRIALS):
        step = (slab_rows[t] // 2 - y_at + 4) % 4
        near = jnp.where(step == 3, 2, step) * 2 + slab_rows[t] % 2
        near = jnp.where(step == 2, -2 * SLABS, near - slab_rows[t])
        place_rows.append(slots[t : t + 1] + (CAP * near).astype(F32))
    slot_columns = 2.0 * jnp.transpose(jnp.concatenate(place_rows, axis=0))
    hot_iota = lax.broadcasted_iota(jnp.int32, (BLOCKS, NEAR * LANES), 1).astype(F32)
    for t in range(TRIALS):
        column = slot_columns[:, t : t + 1]
        hot[t, :BLOCKS, :] = jnp.where(hot_iota == column, 1.0, 0.0).astype(BF16)
        hot[t, BLOCKS:, :] = jnp.where(hot_iota == column + 1.0, 1.0, 0.0).astype(BF16)

    basis[...] = jnp.zeros((8, LANES), F32)
    for i in range(HIST):
        basis[i : i + 1, : 3 * TRIALS] = steps_ref[i]
        basis[HIST + i : HIST + i + 1, : 3 * TRIALS] = changes_ref[i]
    vectors = basis[...]
    gram = jnp.zeros((8, LANES), F32)
    for j in range(8):
        gram = jnp.where(
            lane == j, jnp.sum(vectors * vectors[j : j + 1], axis=1, keepdims=True), gram
        )

    def to_smem(source, peer):
        return pltpu.make_async_copy(source, asked_smem.at[peer], ask_local.at[peer])

    for d in range(1, 8):
        peer = lax.rem(slab + d, 8)
        pltpu.make_async_remote_copy(
            src_ref=asked_out.at[peer],
            dst_ref=asked_in.at[peer],
            send_sem=ask_send.at[peer],
            recv_sem=ask_recv.at[peer],
            device_id=(peer, dom),
            device_id_type=MESH,
        ).wait_recv()
        to_smem(asked_in.at[peer], peer).start()
    to_smem(asked_out.at[slab], slab).start()
    for d in range(1, 8):
        peer = lax.rem(slab + d, 8)
        to_smem(asked_in.at[peer], peer).wait()
    to_smem(asked_out.at[slab], slab).wait()

    def data(peer, u):
        return pltpu.make_async_remote_copy(
            src_ref=sent.at[peer, u],
            dst_ref=landed.at[place_at(peer), u],
            send_sem=data_send.at[peer, u],
            recv_sem=data_recv.at[place_at(peer), u],
            device_id=(peer, dom),
            device_id_type=MESH,
        )

    def pick(peer, u, target):
        for j in range(LANES):
            place = jnp.minimum(jnp.maximum(asked_smem[peer, u, j], 8), row_count + 6)
            target[2 * j : 2 * j + 2, :] = mapped[pl.ds(place, 2), :]

    def pick_trials(u, carry):
        def pick_peer(n, inner):
            step = 1 + 2 * lax.rem(n, 2) - n // 4
            peer = lax.rem(y_at + step, 4) * 2 + n // 2 - (n // 4) * (1 + core)
            pick(peer, u, staged)
            sent[peer, u] = staged[...].astype(BF16)
            data(peer, u).start()
            return inner

        lax.fori_loop(0, 5, pick_peer, 0)
        return carry

    lax.fori_loop(0, 4, pick_trials, 0)

    def pick_own(u, carry):
        pick(slab, u, staged)
        landed[core, u] = staged[...].astype(BF16)
        return carry

    lax.fori_loop(0, 4, pick_own, 0)

    def pick_far(n, carry):
        which, u = n // 4, lax.rem(n, 4)
        pick(lax.rem(slab + 4 + which * (1 - 2 * core), 8), u, kept.at[which, u])
        return carry

    lax.fori_loop(0, 8, pick_far, 0)

    block_iota = lax.broadcasted_iota(jnp.int32, (LANES, BLOCKS), 1).astype(F32)
    slot_lane = lax.broadcasted_iota(jnp.int32, (LANES, LANES), 1)
    slot_first = lax.broadcasted_iota(jnp.int32, (LANES, 1), 0) < CAP
    slot_three = signed(slot_lane % 32)
    for which in range(2):
        far_copy(side_out, side_in, side_sem, which).wait_recv()
        far_copy(info_out, info_in, info_sem, which).wait_recv()
        far_r, far_i = spectrum(info_in[which, :BLOCKS, :])
        far_weight = info_in[which, BLOCKS:, :]
        far_r, far_i = far_r * far_weight.astype(F32), far_i * far_weight.astype(F32)
        high_r, high_i = far_r.astype(BF16), far_i.astype(BF16)
        packed = jnp.concatenate(
            [
                high_r,
                high_i,
                (far_r - high_r.astype(F32)).astype(BF16),
                (far_i - high_i.astype(F32)).astype(BF16),
                far_weight,
            ],
            axis=1,
        )
        far_columns = jnp.transpose(asked_in[far[which]].astype(F32)) - 1.0
        far_shifts = side_in[which]
        for u in range(4):
            column = far_columns[:, 4 + u : 5 + u]
            chosen = dot(jnp.where(block_iota == column, 1.0, 0.0).astype(BF16), packed)
            slot_r = chosen[:, :LANES] + chosen[:, 2 * LANES : 3 * LANES]
            slot_i = chosen[:, LANES : 2 * LANES] + chosen[:, 3 * LANES : 4 * LANES]
            slot_weight = chosen[:, 4 * LANES :]
            block = jnp.maximum(column, 0.0).astype(jnp.int32)
            slot_one = signed(block // 8)
            slot_two = signed(4 * (block % 8) + slot_lane // 32)
            trio = [
                jnp.where(
                    slot_first, far_shifts[u : u + 1, a : a + 1], far_shifts[u + 4 : u + 5, a : a + 1]
                )
                for a in range(3)
            ]
            angle = unit * (slot_one * trio[0] + slot_two * trio[1] + slot_three * trio[2])
            cos_s, sin_s = jnp.cos(angle), jnp.sin(angle)
            row_r = kept[which, u, pl.ds(0, LANES, stride=2), :].astype(BF16).astype(F32)
            row_i = kept[which, u, pl.ds(1, LANES, stride=2), :].astype(BF16).astype(F32)
            cross_r = slot_r * row_r + slot_i * row_i
            cross_i = slot_r * row_i - slot_i * row_r
            real = cross_r * cos_s + cross_i * sin_s
            imag = cross_i * cos_s - cross_r * sin_s
            power = slot_weight * (row_r * row_r + row_i * row_i)
            for n, tile in enumerate(
                (real, imag * slot_one, imag * slot_two, imag * slot_three, power)
            ):
                for half in range(2):
                    t = u + 4 * half
                    partial[n, t : t + 1, :] = jnp.sum(
                        tile[half * CAP : (half + 1) * CAP], axis=0, keepdims=True
                    )
        tile = jnp.zeros((8, LANES), F32)
        for n in range(5):
            tile = jnp.where(lane == n, jnp.sum(partial[n], axis=1, keepdims=True), tile)
        part_out[which] = tile
        far_copy(part_out.at[which], part_in, part_sem, which).start()

    line_copy.wait()

    def correlate(u, carry):
        for d in near_steps:
            peer = lax.rem(slab + d, 8)
            pltpu.make_async_remote_copy(
                src_ref=sent.at[peer, u],
                dst_ref=landed.at[place_of(peer), u],
                send_sem=data_send.at[peer, u],
                recv_sem=data_recv.at[place_of(peer), u],
                device_id=(peer, dom),
                device_id_type=MESH,
            ).wait_recv()
        for half in range(2):
            t = u + 4 * half
            arrived = landed[:, u, half * LANES : (half + 1) * LANES, :]
            box = dot(hot[t], arrived.reshape(NEAR * LANES, LANES))
            zero = jnp.zeros((8, LANES), F32)
            sum_r, sum_i, line_r, line_i, power = zero, zero, zero, zero, zero
            for k in range(EDGE):
                at = slice(8 * k, 8 * k + 8)
                box_r = box[8 * k : 8 * k + 8]
                box_i = box[BLOCKS + 8 * k : BLOCKS + 8 * k + 8]
                spec_r, spec_i, weight = weighted[0, at], weighted[1, at], weighted[2, at]
                cross_r = spec_r * box_r + spec_i * box_i
                cross_i = spec_r * box_i - spec_i * box_r
                cos_k, sin_k = line_smem[0, t, k], line_smem[1, t, k]
                cos_f, sin_f = line_smem[2, t, k], line_smem[3, t, k]
                sum_r = sum_r + (cross_r * cos_k + cross_i * sin_k)
                sum_i = sum_i + (cross_i * cos_k - cross_r * sin_k)
                line_r = line_r + (cross_r * cos_f + cross_i * sin_f)
                line_i = line_i + (cross_i * cos_f - cross_r * sin_f)
                power = power + weight * (box_r * box_r + box_i * box_i)
            cos_t, sin_t = phase_tables[0, t], phase_tables[1, t]
            real = sum_r * cos_t + sum_i * sin_t
            imag = sum_i * cos_t - sum_r * sin_t
            imag_one = line_i * cos_t - line_r * sin_t
            for n, tile in enumerate(
                (real, imag_one, imag * freq_two, imag * freq_three, power)
            ):
                partial[n, pl.ds(t, 1), :] = jnp.sum(tile, axis=0, keepdims=True)
        return carry

    lax.fori_loop(0, 4, correlate, 0)

    for which in range(2):
        far_copy(part_out.at[which], part_in, part_sem, which).wait_recv()
    far_part = part_in[0] + part_in[1]
    totals = [
        jnp.sum(partial[n], axis=1, keepdims=True) + far_part[:, n : n + 1] for n in range(5)
    ]
    factor = math.sqrt(EDGE**3) / jnp.sqrt((power_particle + 1e-06) * (totals[4] + 1e-06))
    scores = jnp.sum(jnp.where(lane == sub, factor * totals[0], 0.0), axis=0, keepdims=True)
    scores_ref[...] = scores[:, :TRIALS]
    active = (1 - flag_ref[0]).astype(F32)
    place = lane - 3 * sub
    slopes = jnp.where(place == 0, totals[1], 0.0)
    slopes = jnp.where(place == 1, totals[2], slopes)
    slopes = jnp.where(place == 2, totals[3], slopes)
    gradient = jnp.sum(-active * (factor * unit) * slopes, axis=0, keepdims=True)
    gram = jnp.where(lane == 8, jnp.sum(vectors * gradient, axis=1, keepdims=True), gram)

    stages = (
        (slab_peers, sum_slab, slab, 0, lambda d: lax.rem(slab + d, 8)),
        (z_peers, sum_z, z_at, 7, lambda d: lax.rem(z_at + d, 8)),
        (x_peers, sum_x, x_at, 14, lambda d: lax.rem(x_at + d, 4)),
    )
    for number, (peers, buffer, own, start, index_of) in enumerate(stages):
        sum_out[number] = gram
        buffer[own] = gram
        size = len(peers) + 1
        for d in range(1, size):
            pltpu.make_async_remote_copy(
                src_ref=sum_out.at[number],
                dst_ref=buffer.at[own],
                send_sem=sum_send.at[start + d - 1],
                recv_sem=sum_recv.at[start + d - 1],
                device_id=peers[d - 1],
                device_id_type=MESH,
            ).start()
        for d in range(1, size):
            pltpu.make_async_remote_copy(
                src_ref=sum_out.at[number],
                dst_ref=buffer.at[index_of(size - d)],
                send_sem=sum_send.at[start + d - 1],
                recv_sem=sum_recv.at[start + d - 1],
                device_id=peers[d - 1],
                device_id_type=MESH,
            ).wait_recv()
        gram = jnp.sum(buffer[...], axis=0)

    lane_row = lane[:1]
    held = jnp.where(lane_row == 2 * HIST, 1.0, 0.0)
    curvature = [gram[i : i + 1, HIST + i : HIST + i + 1] for i in range(HIST)]
    alphas = [None] * HIST
    for i in reversed(range(HIST)):
        alphas[i] = jnp.sum(gram[i : i + 1] * held, axis=1, keepdims=True) / curvature[i]
        held = jnp.where(lane_row == HIST + i, held - alphas[i], held)
    last = 2 * HIST - 1
    gamma = curvature[HIST - 1] / gram[last : last + 1, last : last + 1]
    held = gamma * held
    direction = gradient
    for i in range(HIST):
        direction = direction - alphas[i] * vectors[HIST + i : HIST + i + 1]
    direction = gamma * direction
    for i in range(HIST):
        beta = (
            jnp.sum(gram[HIST + i : HIST + i + 1] * held, axis=1, keepdims=True)
            / curvature[i]
        )
        held = jnp.where(lane_row == i, held + (alphas[i] - beta), held)
        direction = direction + (alphas[i] - beta) * vectors[i : i + 1]
    new_ref[...] = shift_ref[...] - active * direction[:, : 3 * TRIALS]

    for d in range(1, 8):
        ask(lax.rem(slab + d, 8)).wait_send()

    for which in range(2):
        far_copy(side_out, side_in, side_sem, which).wait_send()
        far_copy(info_out, info_in, info_sem, which).wait_send()
        far_copy(part_out.at[which], part_in, part_sem, which).wait_send()

    def drain(u, carry):
        for d in near_steps:
            data(lax.rem(slab + d, 8), u).wait_send()
        return carry

    lax.fori_loop(0, 4, drain, 0)
    for number, (peers, buffer, own, start, index_of) in enumerate(stages):
        for d in range(1, len(peers) + 1):
            pltpu.make_async_remote_copy(
                src_ref=sum_out.at[number],
                dst_ref=buffer.at[own],
                send_sem=sum_send.at[start + d - 1],
                recv_sem=sum_recv.at[start + d - 1],
                device_id=peers[d - 1],
                device_id_type=MESH,
            ).wait_send()


def local(
    reference_blocks,
    corner_maps,
    volumes,
    wedge,
    source_slab,
    block_offset,
    flags,
    shifts,
    past_steps,
    past_changes,
):
    row_count = reference_blocks.shape[0] * 2
    inner_pair, outer_pair, twiddle = transform_tables()
    vmem = pl.BlockSpec(memory_space=pltpu.VMEM)
    smem = pl.BlockSpec(memory_space=pltpu.SMEM)
    hbm = pl.BlockSpec(memory_space=pl.ANY)
    dma = pltpu.SemaphoreType.DMA
    large = (
        reference_blocks.reshape(row_count, LANES),
        corner_maps,
        volumes,
        wedge.reshape(BLOCKS, LANES),
        source_slab.reshape(TRIALS, 1, BLOCKS),
        block_offset.reshape(TRIALS, BLOCKS),
        past_steps,
        past_changes,
        jnp.asarray(inner_pair),
        jnp.asarray(outer_pair),
        jnp.asarray(twiddle),
    )
    return pl.pallas_call(
        step_kernel,
        out_shape=(
            jax.ShapeDtypeStruct((1, TRIALS), F32),
            jax.ShapeDtypeStruct((1, 3 * TRIALS), F32),
        ),
        in_specs=[hbm] * len(large) + [smem, smem, vmem],
        out_specs=(vmem, vmem),
        scratch_shapes=[pltpu.VMEM(a.shape, a.dtype) for a in large]
        + [
            pltpu.VMEM((row_count + 16, LANES), F32),
            pltpu.VMEM((SLABS, 8, LANES), jnp.int32),
            pltpu.VMEM((SLABS, 8, LANES), jnp.int32),
            pltpu.SMEM((SLABS, 8, LANES), jnp.int32),
            pltpu.VMEM((2 * LANES, LANES), F32),
            pltpu.VMEM((2, 4, 2 * LANES, LANES), F32),
            pltpu.VMEM((8, LANES), F32),
            pltpu.VMEM((2, 8, LANES), F32),
            pltpu.VMEM((2 * BLOCKS, LANES), BF16),
            pltpu.VMEM((2, 2 * BLOCKS, LANES), BF16),
            pltpu.VMEM((2, 8, LANES), F32),
            pltpu.VMEM((2, 8, LANES), F32),
            pltpu.VMEM((SLABS, 4, 2 * LANES, LANES), BF16),
            pltpu.VMEM((NEAR, 4, 2 * LANES, LANES), BF16),
            pltpu.VMEM((TRIALS, 2 * BLOCKS, NEAR * LANES), BF16),
            pltpu.VMEM((3, BLOCKS, LANES), F32),
            pltpu.VMEM((2, TRIALS, 8, LANES), F32),
            pltpu.VMEM((4, TRIALS, LANES), F32),
            pltpu.SMEM((4, TRIALS, LANES), F32),
            pltpu.VMEM((5, TRIALS, LANES), F32),
            pltpu.VMEM((8, LANES), F32),
            pltpu.VMEM((8, 8, LANES), F32),
            pltpu.VMEM((8, 8, LANES), F32),
            pltpu.VMEM((4, 8, LANES), F32),
            pltpu.VMEM((3, 8, LANES), F32),
            dma((11,)),
            dma((8,)),
            dma((8,)),
            dma((8,)),
            dma((8, 4)),
            dma((NEAR, 4)),
            dma((2, 2)),
            dma((2, 2)),
            dma((2, 2)),
            dma,
            dma((17,)),
            dma((17,)),
        ],
        compiler_params=pltpu.CompilerParams(
            collective_id=0, has_side_effects=True, vmem_limit_bytes=56 * 2**20
        ),
    )(*large, flags, shifts, shifts)


def solution(mesh):
    return jax.shard_map(
        local,
        mesh=mesh,
        in_specs=(
            P("slab", None, None),
            P(),
            P(("slab", "dom"), None, None, None),
            P(("slab", "dom"), None),
            P(("slab", "dom"), None, None, None),
            P(("slab", "dom"), None, None),
            P(("slab", "dom")),
            P(("slab", "dom"), None),
            P(None, ("slab", "dom"), None),
            P(None, ("slab", "dom"), None),
        ),
        out_specs=(P(("slab", "dom"), None), P(("slab", "dom"), None)),
        check_vma=False,
    )
```
